32 devices in a mesh: prow: 4 (over x, core), pcol: 8 (over z, y).
Axes of the slice: x: 2, y: 2, z: 4, core: 2. Of those that a mesh axis runs over, the one named last changes fastest.
Arguments:
- basis: bfloat16 [512, 256], replicated, may hold values from -0.25 to 0.25
- potentials: float32 [8, 512], replicated, may hold values from -6 to 6
- orbitals: bfloat16 [64, 512], P('pcol'), may hold values from -6 to 6
- chan_orbital: int32 [128], replicated, may hold values from 0 to 63
- pair_list: int32 [6144, 3], P(('prow', 'pcol')), may hold values from 0 to 127, as said below
- slot_list: int32 [6144], P(('prow', 'pcol')), may hold values from 0 to 63
- coefs: float32 [6144, 2], P(('prow', 'pcol')), may hold values from -6 to 6
- exchange_ops: bfloat16 [6144, 128, 256], P(('prow', 'pcol')), may hold values from -1.1953125 to 1.1953125
Outputs:
- hamiltonian: bfloat16 [32, 4, 2, 8, 256, 256], P(None, 'prow', None, 'pcol')
The draws below stay inside these ranges and needn't reach their ends.
Inputs may be any that keep to these rules, and one draw needn't show every extreme that they name: `pair_list`: columns 0 and 1 are channels a, b; column 2 is a multipole order below 8. (b // 8 - a // 8) modulo 128 // 8 is below 2. Terms of one device with the same slot s have the same two channels, and the block (a, b) belongs to owner s // 2 in prow-major order: a % 4 and b % 8 are that owner's prow and pcol indices.
All inputs are finite; a program needn't handle non-finite values.
Results may differ from the reference program's by a relative error of at most 0.0058.
Values may be sent and summed in bfloat16 or wider, within the bound.
A program may use at most 320 MiB of HBM per device.

```python
import jax
import jax.numpy as jnp
from jax import lax

NB = 256
NQ = 512
NQX = 128
NORB = 64
LAM = 8
CAP = 2
BAND = 2
RBLK = 32
EDEV = 192
CHAN = 128
SLOTS = 64
ENTRIES = 6144
N_PROW = 4
N_PCOL = 8
DEVICES = 32


def common_lists(key):
    order_key = jax.random.fold_in(key, 11)
    block_key = jax.random.fold_in(key, 23)
    multipole_key = jax.random.fold_in(key, 37)
    repeat_key = jax.random.fold_in(key, 41)
    device_keys = jax.random.split(order_key, DEVICES)
    slot_orders = jax.vmap(lambda device_key: jax.random.permutation(device_key, SLOTS))(device_keys).astype(jnp.int32)
    distinct = min(EDEV * 2 // 3, SLOTS)
    term_range = jnp.arange(EDEV, dtype=jnp.int32)
    repeats = jax.random.randint(repeat_key, (DEVICES, EDEV), 0, distinct, dtype=jnp.int32)
    positions = jnp.where(term_range[None, :] < distinct, term_range[None, :], repeats).astype(jnp.int32)
    slot_table = jnp.take_along_axis(slot_orders, positions, axis=1)
    slot_table = slot_table.at[:, EDEV - 1].set(SLOTS - 1)
    block_table = jax.random.randint(block_key, (DEVICES, SLOTS), 0, RBLK * BAND, dtype=jnp.int32)
    chosen = jnp.take_along_axis(block_table, slot_table, axis=1)
    owner_index = slot_table // CAP
    owner_row = owner_index // N_PCOL
    owner_col = owner_index % N_PCOL
    col_groups = CHAN // N_PCOL
    first_chan = chosen // BAND * N_PROW + owner_row
    col_group = jnp.mod(first_chan // N_PCOL + chosen % BAND, col_groups)
    second_chan = col_group * N_PCOL + owner_col
    multipole = jax.random.randint(multipole_key, (DEVICES, EDEV), 0, LAM, dtype=jnp.int32)
    pair_rows = jnp.stack([first_chan, second_chan, multipole], axis=-1).reshape(ENTRIES, 3)
    return (pair_rows.astype(jnp.int32), slot_table.reshape(ENTRIES).astype(jnp.int32))


def draw_pair_list(key, part):
    return common_lists(key)[0]


def draw_slot_list(key, part):
    return common_lists(key)[1]


def set_ends(values, stream_key, smallest, high):
    longest = values.shape.index(max(values.shape))
    spots = []
    for shift in (0, 1):
        where = [jax.random.randint(jax.random.fold_in(stream_key, axis), (), 0, length) for axis, length in enumerate(values.shape)]
        where[longest] = (where[longest] + shift) % values.shape[longest]
        spots.append(tuple(where))
    return values.at[spots[0]].set(smallest).at[spots[1]].set(high)


def shard_levels(key, dims, pieces, smallest, top_value):
    level = 1.0
    for dim, blocks in pieces:
        heights = jax.random.uniform(jax.random.fold_in(jax.random.fold_in(key, 6), dim), (blocks,), jnp.float32, smallest / len(pieces), top_value / len(pieces))
        level = level * jnp.repeat(jnp.exp(heights), dims[dim] // blocks).reshape((-1,) + (1,) * (len(dims) - 1 - dim))
    return level


def normal_values(key, dims, scale, reach, cuts=(), kind=jnp.bfloat16):
    array = scale * jax.random.normal(key, dims, jnp.float32)
    if cuts:
        array = array * shard_levels(key, dims, cuts, -0.22, 0.18)
    return jnp.clip(array, -reach, reach).astype(kind)


def setup_inputs(seed: int = 0) -> dict:
    key_list = jax.random.split(jax.random.key(seed), 9)
    return {
        "basis": normal_values(key_list[0], (NQ, NB), NQ ** -0.5, 0.25),
        "potentials": normal_values(key_list[1], (LAM, NQ), 1.0, 6.0, (), jnp.float32),
        "orbitals": normal_values(key_list[2], (NORB, NQ), 1.0, 6.0, ((0, 8),)),
        "chan_orbital": set_ends(jax.random.randint(key_list[3], (CHAN,), 0, NORB), jax.random.fold_in(key_list[3], 1), 0, NORB - 1).astype(jnp.int32),
        "pair_list": draw_pair_list(jax.random.fold_in(key_list[8], 71), 0),
        "slot_list": draw_slot_list(jax.random.fold_in(key_list[8], 71), 0),
        "coefs": normal_values(key_list[6], (ENTRIES, 2), 1.0, 6.0, ((0, 32),), jnp.float32),
        "exchange_ops": normal_values(key_list[7], (ENTRIES, NQX, NB), 0.2, 1.1953125, ((0, 32),)),
    }


def build_tiles(weights_group, exchange_group, basis):
    weights_group, exchange_group = lax.optimization_barrier((weights_group, exchange_group))
    basis_float = basis.astype(jnp.float32)
    scaled = (weights_group.astype(jnp.float32)[:, :, None] * basis_float[None]).astype(jnp.bfloat16)
    scaled = lax.optimization_barrier(scaled)
    inner_rows = basis_float[:exchange_group.shape[1]]
    local_part = jnp.einsum('qa,gqb->gab', basis_float, scaled.astype(jnp.float32))
    exchange_part = jnp.einsum('qa,gqb->gab', inner_rows, exchange_group.astype(jnp.float32))
    return (local_part + exchange_part).astype(jnp.bfloat16)


def reference(basis, potentials, orbitals, chan_orbital, pair_list, slot_list, coefs, exchange_ops):
    orb_float = orbitals.astype(jnp.float32)
    col_groups = CHAN // N_PCOL
    block_count = RBLK * BAND
    dropped = DEVICES * block_count

    def add_device(carried, device_index):
        first_term = (device_index * EDEV).astype(jnp.int32)
        pair_rows = lax.dynamic_slice_in_dim(pair_list, first_term, EDEV, 0)
        term_slots = lax.dynamic_slice_in_dim(slot_list, first_term, EDEV, 0)
        factors = lax.dynamic_slice_in_dim(coefs, first_term, EDEV, 0)
        operands = lax.dynamic_slice_in_dim(exchange_ops, first_term, EDEV, 0)
        first_chan = pair_rows[:, 0]
        second_chan = pair_rows[:, 1]
        multipole = pair_rows[:, 2]
        first_orb = chan_orbital[first_chan]
        second_orb = chan_orbital[second_chan]
        radial = factors[:, 0:1] * potentials[multipole] + factors[:, 1:2] * (orb_float[first_orb] * orb_float[second_orb])
        slot_weight = jax.ops.segment_sum(radial, term_slots, num_segments=SLOTS).astype(jnp.bfloat16)
        slot_exchange = jax.ops.segment_sum(operands.astype(jnp.float32), term_slots, num_segments=SLOTS).astype(jnp.bfloat16)
        offset = jnp.mod(second_chan // N_PCOL - first_chan // N_PCOL, col_groups)
        block_index = ((first_chan // N_PROW) * BAND + offset).astype(jnp.int32)
        slot_ids = jax.ops.segment_max(block_index, term_slots, num_segments=SLOTS)
        owner_index = jnp.arange(SLOTS, dtype=jnp.int32) // CAP
        global_ids = jnp.where(slot_ids >= 0, owner_index * block_count + slot_ids, dropped).astype(jnp.int32)
        built_tiles = build_tiles(slot_weight, slot_exchange, basis)
        carried = carried.at[global_ids].add(built_tiles.astype(jnp.float32), mode="drop")
        return carried, None

    zeros_start = jnp.zeros((DEVICES * block_count, NB, NB), jnp.float32)
    summed_blocks, unused = lax.scan(add_device, zeros_start, jnp.arange(DEVICES, dtype=jnp.int32))
    blocks = summed_blocks.astype(jnp.bfloat16).reshape(N_PROW, N_PCOL, RBLK, BAND, NB, NB)
    return jnp.transpose(blocks, (2, 0, 3, 1, 4, 5))
```

```python
import functools

import jax
import jax.numpy as jnp
from jax import lax
from jax.experimental import pallas as pl
from jax.experimental.pallas import tpu as pltpu
from jax.sharding import PartitionSpec as P

CAP = 2
BAND = 2
RBLK = 32
TERMS_STEP = 16
BLOCKS_STEP = 8
PACK = 16
VMEM_BYTES = 56 * 1024 * 1024
MESH = pl.DeviceIdType.MESH


def sum_slots_kernel(slot_smem, ops_ref, out_ref, acc):
    step = pl.program_id(0)
    slots = acc.shape[0]

    @pl.when(step == 0)
    def _():
        def clear(s, c):
            acc[s] = jnp.zeros(acc.shape[1:], jnp.float32)
            return c

        lax.fori_loop(0, slots, clear, 0)

    for i in range(TERMS_STEP):
        s = slot_smem[step * TERMS_STEP + i]
        acc[s] += ops_ref[i].astype(jnp.float32)

    @pl.when(step == pl.num_programs(0) - 1)
    def _():
        def convert(s, c):
            out_ref[s] = acc[s].astype(jnp.bfloat16)
            return c

        lax.fori_loop(0, slots, convert, 0)


def sum_slots(slot_list, exchange_ops, slot_count):
    terms, inner, width = exchange_ops.shape
    return pl.pallas_call(
        sum_slots_kernel,
        grid_spec=pltpu.PrefetchScalarGridSpec(
            num_scalar_prefetch=1,
            grid=(terms // TERMS_STEP,),
            in_specs=[pl.BlockSpec((TERMS_STEP, inner, width), lambda i, s: (i, 0, 0))],
            out_specs=pl.BlockSpec((slot_count, inner, width), lambda i, s: (0, 0, 0)),
            scratch_shapes=[pltpu.VMEM((slot_count, inner, width), jnp.float32)],
        ),
        out_shape=jax.ShapeDtypeStruct((slot_count, inner, width), jnp.bfloat16),
        compiler_params=pltpu.CompilerParams(
            dimension_semantics=("arbitrary",), vmem_limit_bytes=VMEM_BYTES
        ),
        name="sum_slots",
    )(slot_list, exchange_ops)


def exchange_kernel(
    nrow,
    ncol,
    col_groups,
    orb_per,
    exch_ref,
    orb_ref,
    pot_ref,
    chan_ref,
    rows_ref,
    pair_ref,
    coef_ref,
    recv_ref,
    wrecv_ref,
    all_orb,
    wsend,
    orb_ssem,
    orb_rsem,
    w_ssem,
    w_rsem,
    e_ssem,
    e_rsem,
    own_sem,
):
    p = lax.axis_index("prow")
    q = lax.axis_index("pcol")
    ndev = nrow * ncol
    me = p * ncol + q
    f32 = jnp.float32

    def peer(t):
        dq = lax.rem(t * (ncol // 2 + 1), ncol)
        dp = lax.rem(lax.div(t, ncol) + t, nrow)
        return lax.rem(p + dp, nrow), lax.rem(q + dq, ncol)

    barrier = pltpu.get_barrier_semaphore()

    def greet(t, c):
        pp, qq = peer(t)
        pl.semaphore_signal(barrier, inc=1, device_id=(pp, qq), device_id_type=MESH)
        return c

    lax.fori_loop(1, ndev, greet, 0)
    pl.semaphore_wait(barrier, ndev - 1)

    def orb_copy(t):
        return pltpu.make_async_remote_copy(
            src_ref=orb_ref,
            dst_ref=all_orb.at[q],
            send_sem=orb_ssem.at[t],
            recv_sem=orb_rsem.at[t],
            device_id=(p, lax.rem(q + t, ncol)),
            device_id_type=MESH,
        )

    def exch_copy(t):
        pp, qq = peer(t)
        return pltpu.make_async_remote_copy(
            src_ref=exch_ref.at[pp * ncol + qq],
            dst_ref=recv_ref.at[me],
            send_sem=e_ssem.at[t],
            recv_sem=e_rsem.at[t],
            device_id=(pp, qq),
            device_id_type=MESH,
        )

    def weight_copy(t):
        pp, qq = peer(t)
        return pltpu.make_async_remote_copy(
            src_ref=wsend.at[pp * ncol + qq],
            dst_ref=wrecv_ref.at[me],
            send_sem=w_ssem.at[t],
            recv_sem=w_rsem.at[t],
            device_id=(pp, qq),
            device_id_type=MESH,
        )

    def each(count, action):
        def body(t, c):
            action(t)
            return c

        lax.fori_loop(1, count, body, 0)

    each(ncol, lambda t: orb_copy(t).start())
    each(ndev, lambda t: exch_copy(t).start())
    own = pltpu.make_async_copy(exch_ref.at[me], recv_ref.at[me], own_sem.at[0])
    own.start()
    each(ncol, lambda t: orb_copy(t).wait())
    all_orb[q] = orb_ref[...]

    terms = pair_ref.shape[0]
    points = orb_ref.shape[1]
    chans = chan_ref.shape[1]
    orbs = all_orb[...].reshape(ncol * all_orb.shape[1], points).astype(jnp.bfloat16)
    chan_iota = lax.broadcasted_iota(jnp.int32, (terms, chans), 1)
    orb_iota = lax.broadcasted_iota(jnp.int32, (terms, orbs.shape[0]), 1)

    def pick(column):
        chan = pair_ref[:, column : column + 1]
        orb = jnp.sum(jnp.where(chan_iota == chan, chan_ref[...], 0), axis=1, keepdims=True)
        place = orb // orb_per * all_orb.shape[1] + orb % orb_per
        hot = jnp.where(orb_iota == place, 1.0, 0.0).astype(jnp.bfloat16)
        return jnp.dot(hot, orbs, preferred_element_type=f32)

    pot = jnp.zeros((terms, points), f32)
    multipole = pair_ref[:, 2:3]
    for l in range(pot_ref.shape[0]):
        pot = jnp.where(multipole == l, pot_ref[l : l + 1, :], pot)
    radial = coef_ref[:, 0:1] * pot + coef_ref[:, 1:2] * (pick(0) * pick(1))

    pieces = points // 128
    lines = ndev * PACK
    line = lax.broadcasted_iota(jnp.int32, (lines, terms), 0)
    inside = line % PACK
    line_slot = line // PACK * CAP + inside % (CAP * pieces) // pieces
    match = line_slot == rows_ref[0:1, :]
    is_weight = inside < CAP * pieces
    total = jnp.zeros((lines, 128), f32)
    for j in range(pieces):
        hot = jnp.where(match & is_weight & (inside % pieces == j), 1.0, 0.0).astype(f32)
        total += jnp.dot(
            hot,
            radial[:, j * 128 : (j + 1) * 128],
            precision=lax.Precision.HIGHEST,
            preferred_element_type=f32,
        )
    first = rows_ref[1:2, :]
    second = rows_ref[2:3, :]
    offset = (second // ncol - first // ncol + col_groups) % col_groups
    block = (first // nrow * BAND + offset).astype(f32)
    ids = jnp.max(jnp.where(match, block, -1.0), axis=1, keepdims=True)
    line_col = lax.broadcasted_iota(jnp.int32, (lines, 128), 0) % PACK
    total = jnp.where(line_col < CAP * pieces, total, ids)
    wsend[...] = total.astype(jnp.bfloat16).reshape(ndev, PACK, 128)

    each(ndev, lambda t: weight_copy(t).start())
    own_w = pltpu.make_async_copy(wsend.at[me], wrecv_ref.at[me], own_sem.at[1])
    own_w.start()
    each(ndev, lambda t: exch_copy(t).wait())
    each(ndev, lambda t: weight_copy(t).wait())
    own.wait()
    own_w.wait()


def exchange(nrow, ncol, col_groups, slot_sums, orb, potentials, chan, rows, pairs, coefs, orb_per):
    ndev = nrow * ncol
    inner, width = slot_sums.shape[1:]
    any_spec = pl.BlockSpec(memory_space=pl.ANY)
    vmem = pl.BlockSpec(memory_space=pltpu.VMEM)
    dma = pltpu.SemaphoreType.DMA
    return pl.pallas_call(
        functools.partial(exchange_kernel, nrow, ncol, col_groups, orb_per),
        out_shape=(
            jax.ShapeDtypeStruct((ndev, CAP, inner, width), jnp.bfloat16),
            jax.ShapeDtypeStruct((ndev, PACK, 128), jnp.bfloat16),
        ),
        in_specs=[any_spec] + [vmem] * 6,
        out_specs=(any_spec, any_spec),
        scratch_shapes=[
            pltpu.VMEM((ncol,) + orb.shape, jnp.float32),
            pltpu.VMEM((ndev, PACK, 128), jnp.bfloat16),
            dma((ncol,)),
            dma((ncol,)),
            dma((ndev,)),
            dma((ndev,)),
            dma((ndev,)),
            dma((ndev,)),
            dma((2,)),
        ],
        compiler_params=pltpu.CompilerParams(
            collective_id=0, has_side_effects=True, vmem_limit_bytes=VMEM_BYTES
        ),
        name="exchange",
    )(slot_sums.reshape(ndev, CAP, inner, width), orb, potentials, chan, rows, pairs, coefs)


def blocks_kernel(
    ids_smem, recv_ref, wrecv_ref, basis_ref, basis_t_ref, out_ref, weights, heads, nexts, sums
):
    step = pl.program_id(0)
    slots = recv_ref.shape[0]
    blocks = heads.shape[0]
    inner, width = recv_ref.shape[1:]
    ndev = wrecv_ref.shape[0]
    pieces = basis_ref.shape[0] // 128
    half = CAP * pieces
    f32 = jnp.float32

    @pl.when(step == 0)
    def _():
        def clear(t, c):
            heads[t] = -1
            return c

        lax.fori_loop(0, blocks, clear, 0)

        def link(s, c):
            t = ids_smem[s]

            @pl.when(t >= 0)
            def _():
                nexts[s] = heads[t]
                heads[t] = s

            return c

        lax.fori_loop(0, slots, link, 0)
        packed = wrecv_ref[...].astype(f32)
        values = packed[:, :half, :].reshape(ndev * half, 128).astype(jnp.bfloat16)
        ids = packed[:, half:, :].reshape(ndev * half, 128)
        lane = lax.broadcasted_iota(jnp.int32, ids.shape, 1).astype(f32)
        piece = lax.broadcasted_iota(jnp.int32, ids.shape, 0) % pieces
        for j in range(pieces):
            hot = jnp.where((ids == lane) & (piece == j), 1.0, 0.0).astype(jnp.bfloat16)
            weights[:, j * 128 : (j + 1) * 128] = lax.dot_general(
                hot, values, (((0,), (0,)), ((), ())), preferred_element_type=f32
            )[:blocks]

    for i in range(BLOCKS_STEP):
        t = step * BLOCKS_STEP + i
        head = heads[t]

        @pl.when(head < 0)
        def _():
            out_ref[i] = jnp.zeros(out_ref.shape[1:], out_ref.dtype)

        @pl.when(head >= 0)
        def _():
            sums[...] = recv_ref[head].astype(f32)

            def more(s):
                sums[...] += recv_ref[s].astype(f32)
                return nexts[s]

            lax.while_loop(lambda s: s >= 0, more, nexts[head])
            scaled = (basis_t_ref[...].astype(f32) * weights[pl.ds(t, 1), :]).astype(jnp.bfloat16)
            local = jnp.dot(scaled, basis_ref[...], preferred_element_type=f32)
            swapped = jnp.dot(
                basis_t_ref[:, :inner], sums[...].astype(jnp.bfloat16), preferred_element_type=f32
            )
            out_ref[i] = (local + swapped).astype(out_ref.dtype)


def make_blocks(ids, received, packed, basis, basis_t):
    slots, inner, width = received.shape
    blocks = RBLK * BAND
    points = basis.shape[0]
    whole = lambda a: pl.BlockSpec(a.shape, lambda i, s: (0,) * a.ndim)
    return pl.pallas_call(
        blocks_kernel,
        grid_spec=pltpu.PrefetchScalarGridSpec(
            num_scalar_prefetch=1,
            grid=(blocks // BLOCKS_STEP,),
            in_specs=[whole(received), whole(packed), whole(basis), whole(basis_t)],
            out_specs=pl.BlockSpec((BLOCKS_STEP, width, width), lambda i, s: (i, 0, 0)),
            scratch_shapes=[
                pltpu.VMEM((blocks, points), jnp.float32),
                pltpu.SMEM((blocks,), jnp.int32),
                pltpu.SMEM((slots,), jnp.int32),
                pltpu.VMEM((inner, width), jnp.float32),
            ],
        ),
        out_shape=jax.ShapeDtypeStruct((blocks, width, width), jnp.bfloat16),
        compiler_params=pltpu.CompilerParams(
            dimension_semantics=("arbitrary",), vmem_limit_bytes=VMEM_BYTES
        ),
        name="make_blocks",
    )(ids, received, packed, basis, basis_t)


def on_device(basis, potentials, orbitals, chan_orbital, pair_list, slot_list, coefs, exchange_ops):
    nrow = lax.axis_size("prow")
    ncol = lax.axis_size("pcol")
    slot_count = nrow * ncol * CAP
    inner, width = exchange_ops.shape[1:]
    orb_per = orbitals.shape[0]
    padding = -orb_per % 8
    orb = jnp.pad(orbitals.astype(jnp.float32), ((0, padding), (0, 0)))
    rows = jnp.concatenate([slot_list[None, :], pair_list.T], axis=0)
    slot_sums = sum_slots(slot_list, exchange_ops, slot_count)
    received, packed = exchange(
        nrow,
        ncol,
        chan_orbital.shape[0] // ncol,
        slot_sums,
        orb,
        potentials,
        chan_orbital[None, :],
        rows,
        pair_list,
        coefs,
        orb_per,
    )
    pieces = basis.shape[0] // 128
    ids = packed[:, CAP * pieces :: pieces, 0].astype(jnp.int32).reshape(slot_count)
    blocks = make_blocks(ids, received.reshape(slot_count, inner, width), packed, basis, basis.T)
    return blocks.reshape(RBLK, 1, BAND, 1, width, width)


def solution(mesh):
    placed = (
        P(),
        P(),
        P("pcol", None),
        P(),
        P(("prow", "pcol"), None),
        P(("prow", "pcol")),
        P(("prow", "pcol"), None),
        P(("prow", "pcol"), None, None),
    )
    return jax.shard_map(
        on_device,
        mesh=mesh,
        in_specs=placed,
        out_specs=P(None, "prow", None, "pcol", None, None),
        check_vma=False,
    )
```

```python
import functools

import jax
import jax.numpy as jnp
from jax import lax
from jax.experimental import pallas as pl
from jax.experimental.pallas import tpu as pltpu
from jax.sharding import PartitionSpec as P

CAP = 2
BAND = 2
RBLK = 32
BLOCKS_STEP = 8
FIRST_ROWS = 32
SPAN = 16
VMEM_BYTES = 56 * 1024 * 1024
MESH = pl.DeviceIdType.MESH
EXACT = lax.Precision.HIGHEST
FAR = 1.0e6


def product(left, right, left_dim, right_dim, precision=None):
    return lax.dot_general(
        left,
        right,
        (((left_dim,), (right_dim,)), ((), ())),
        precision=precision,
        preferred_element_type=jnp.float32,
    )


def iota(shape, dim):
    return lax.broadcasted_iota(jnp.int32, shape, dim)


def turned(row):
    n = row.shape[1]
    same = iota((n, n), 0) == iota((n, n), 1)
    return jnp.sum(jnp.where(same, row, jnp.zeros_like(row)), axis=1, keepdims=True)


def slot_order(slot, slots, table):
    n = slot.shape[1]
    col = turned(slot)
    under, over = iota((n, n), 0), iota((n, n), 1)
    same = col == slot
    rank = jnp.sum(jnp.where((col < slot) | (same & (under < over)), 1, 0), axis=0, keepdims=True)
    place = turned(rank) == over
    before = jnp.sum(jnp.where(same & (over < under), 1, 0), axis=1, keepdims=True)
    order = jnp.sum(jnp.where(place, under, 0), axis=0, keepdims=True)
    keeps = jnp.sum(jnp.where(place, before, 0), axis=0, keepdims=True)
    upto = jnp.where(col <= iota((n, slots), 1), 1, 0)
    last = jnp.sum(upto, axis=0, keepdims=True) - 1
    table[...] = jnp.zeros_like(table)
    table[0:1, :n] = order
    table[1:2, :n] = keeps
    table[2:3, :slots] = last


def exchange_kernel(
    nrow,
    ncol,
    ops_ref,
    orb_ref,
    pot_ref,
    chan_ref,
    slot_ref,
    pair_ref,
    coef_ref,
    basis_ref,
    recv_ref,
    local_ref,
    lists_ref,
    terms_a,
    terms_b,
    running,
    send_a,
    send_b,
    orb_wide,
    orb_send,
    all_orb,
    msg_send,
    msg_recv,
    pot_pad,
    basis_t,
    weights,
    local_blocks,
    table,
    order_smem,
    orb_ssem,
    orb_rsem,
    m_ssem,
    m_rsem,
    e_ssem,
    e_rsem,
    own_sem,
):
    p = lax.axis_index("prow")
    q = lax.axis_index("pcol")
    ndev = nrow * ncol
    me = p * ncol + q
    f32 = jnp.float32
    bf16 = jnp.bfloat16
    slots = ndev * CAP
    blocks = RBLK * BAND
    terms = slot_ref.shape[1]
    chans = chan_ref.shape[1]
    groups = chans // ncol
    points = pot_ref.shape[1]
    orb_per = orb_ref.shape[0]
    orb_rows = orb_wide.shape[0]
    top = terms - 1
    chunks = ((terms_a, send_a, 0), (terms_b, send_b, FIRST_ROWS))

    def peer(t):
        dq = lax.rem(t * (ncol // 2 + 1), ncol)
        dp = lax.rem(lax.div(t, ncol) + t, nrow)
        return lax.rem(p + dp, nrow), lax.rem(q + dq, ncol)

    def each(count, action):
        def body(t, c):
            action(t)
            return c

        lax.fori_loop(1, count, body, 0)

    def load(c):
        buffer, _, start = chunks[c]
        return pltpu.make_async_copy(
            ops_ref.at[:, pl.ds(start, buffer.shape[1]), :], buffer, own_sem.at[c]
        )

    def remote(source, target, sems, t, device):
        return pltpu.make_async_remote_copy(
            src_ref=source,
            dst_ref=target,
            send_sem=sems[0].at[t],
            recv_sem=sems[1].at[t],
            device_id=device,
            device_id_type=MESH,
        )

    def orb_copy(t):
        return remote(
            orb_send, all_orb.at[q], (orb_ssem, orb_rsem), t, (p, lax.rem(q + t, ncol))
        )

    def msg_copy(t):
        pp, qq = peer(t)
        return remote(
            msg_send.at[pp * ncol + qq], msg_recv.at[me], (m_ssem, m_rsem), t, (pp, qq)
        )

    def landing(c):
        _, send, start = chunks[c]
        return recv_ref.at[me, :, pl.ds(start, send.shape[2]), :]

    def exch_copy(c, t):
        pp, qq = peer(t)
        return remote(
            chunks[c][1].at[pp * ncol + qq],
            landing(c),
            (e_ssem.at[c], e_rsem.at[c]),
            t,
            (pp, qq),
        )

    def own_copy(c):
        return pltpu.make_async_copy(chunks[c][1].at[me], landing(c), own_sem.at[2 + c])

    load(0).start()
    load(1).start()
    barrier = pltpu.get_barrier_semaphore()
    each(
        ndev,
        lambda t: pl.semaphore_signal(barrier, inc=1, device_id=peer(t), device_id_type=MESH),
    )

    orb_wide[...] = jnp.zeros_like(orb_wide)
    orb_wide[:orb_per, :] = orb_ref[...].astype(f32)
    orb_send[...] = jnp.concatenate(
        [orb_wide[:, : points // 2], orb_wide[:, points // 2 :]], axis=0
    ).astype(bf16)

    slot = slot_ref[...]
    first, second, multipole = pair_ref[0:1, :], pair_ref[1:2, :], pair_ref[2:3, :]
    offset = (second // ncol - first // ncol + groups) % groups
    block = (first // nrow * BAND + offset).astype(f32)
    kind = iota((128, terms), 0)
    lane = iota((ndev, 128), 1)
    message = jnp.zeros((ndev, 128), f32)
    for c in range(CAP):
        base = SPAN * c
        parts = jnp.where(kind == multipole + base, coef_ref[0:1, :], 0.0)
        parts = jnp.where(kind == base + 8, coef_ref[1:2, :], parts)
        match = slot == iota((ndev, terms), 0) * CAP + c
        message += product(jnp.where(match, 1.0, 0.0), parts, 1, 1, EXACT)
        number = jnp.max(jnp.where(match, block, -1.0), axis=1, keepdims=True)
        message = jnp.where(lane == base + 9, number, message)
    msg_send[...] = message.reshape(ndev, 1, 128)

    slot_order(slot, slots, table)
    order_copy = pltpu.make_async_copy(table, order_smem, own_sem.at[4])
    order_copy.start()
    pl.semaphore_wait(barrier, ndev - 1)
    each(ncol, lambda t: orb_copy(t).start())
    each(ndev, lambda t: msg_copy(t).start())
    order_copy.wait()

    for c, (buffer, send, _) in enumerate(chunks):
        height, width = buffer.shape[1:]
        load(c).wait()

        def add(i, total):
            kept = jnp.where(order_smem[1, i] > 0, total, jnp.zeros_like(total))
            total = kept + buffer[jnp.clip(order_smem[0, i], 0, top)].astype(f32)
            running[i, :height, :] = total.astype(bf16)
            return total

        lax.fori_loop(0, terms, add, jnp.zeros((height, width), f32), unroll=4)

        def place(o, carried):
            for k in range(CAP):
                end = jnp.clip(order_smem[2, o * CAP + k], 0, top)
                send[o, k] = running[end, :height, :]
            return carried

        lax.fori_loop(0, ndev, place, 0)
        each(ndev, lambda t: exch_copy(c, t).start())
        own_copy(c).start()

    each(ncol, lambda t: orb_copy(t).wait())
    all_orb[q] = orb_send[...]
    each(ndev, lambda t: msg_copy(t).wait())
    msg_recv[me] = msg_send[me]

    wide = all_orb[...].astype(f32)
    orbs = jnp.concatenate(
        [
            wide[:, :orb_rows, :].reshape(ncol * orb_rows, points // 2),
            wide[:, orb_rows:, :].reshape(ncol * orb_rows, points // 2),
        ],
        axis=1,
    ).astype(bf16)
    chan_row = chan_ref[...]
    chan_place = chan_row // orb_per * orb_rows + chan_row % orb_per
    owns = jnp.where(iota((ncol * orb_rows, chans), 0) == chan_place, 1.0, 0.0).astype(bf16)
    number = iota((128, chans), 0)
    first_chan = number // BAND * nrow + p
    second_chan = (first_chan // ncol + number % BAND) % groups * ncol + q

    def orbital_of(chan):
        hot = jnp.where(iota((128, chans), 1) == chan, 1.0, 0.0).astype(bf16)
        return product(product(hot, owns, 1, 1).astype(bf16), orbs, 1, 0)

    received = msg_recv[...].reshape(ndev, 128)
    numbers = []
    sums = jnp.zeros((128, 128), f32)
    for c in range(CAP):
        base = SPAN * c
        ids = jnp.sum(jnp.where(lane == base + 9, received, 0.0), axis=1, keepdims=True)
        numbers.append(ids)
        hot = jnp.where(lane.astype(f32) == ids, 1.0, 0.0)
        inside = (lane >= base) & (lane < base + 9)
        sums += product(hot, jnp.where(inside, received, 0.0), 0, 0, EXACT)
    pot_pad[...] = jnp.zeros_like(pot_pad)
    for c in range(CAP):
        pot_pad[SPAN * c : SPAN * c + 8, :] = pot_ref[...]
    lanes = iota((128, 128), 1)
    factor = jnp.sum(jnp.where(lanes % SPAN == 8, sums, 0.0), axis=1, keepdims=True)
    weights[...] = product(sums, pot_pad[...], 1, 0, EXACT) + factor * (
        orbital_of(first_chan) * orbital_of(second_chan)
    )

    size = lists_ref.shape[1]
    source = iota((ndev, size), 0)
    spot = iota((ndev, size), 1)
    row = jnp.full((1, size), -1.0, f32)
    for c in range(CAP):
        row += jnp.sum(
            jnp.where(spot == source * CAP + c, numbers[c] + 1.0, 0.0), axis=0, keepdims=True
        )
    col = turned(row)
    under = iota((size, size), 0).astype(f32)
    over = iota((size, size), 1).astype(f32)
    heads = jnp.min(jnp.where(col == over, under, FAR), axis=0, keepdims=True)
    nexts = jnp.min(jnp.where((col == row) & (under > over), under, FAR), axis=0, keepdims=True)
    lists_ref[...] = jnp.zeros_like(lists_ref)
    lists_ref[0:1, :] = jnp.where(heads < FAR, heads, -1.0).astype(jnp.int32)
    lists_ref[1:2, :] = jnp.where(nexts < FAR, nexts, -1.0).astype(jnp.int32)

    basis_t[...] = basis_ref[...].astype(f32).T

    def form(t, carried):
        scaled = (basis_t[...] * weights[pl.ds(t, 1), :]).astype(bf16)
        local_blocks[t] = jnp.dot(
            scaled, basis_ref[...], preferred_element_type=f32
        ).astype(bf16)
        return carried

    lax.fori_loop(0, blocks, form, 0)
    out_copy = pltpu.make_async_copy(local_blocks, local_ref, own_sem.at[5])
    out_copy.start()
    for c in range(len(chunks)):
        each(ndev, lambda t: exch_copy(c, t).wait())
        own_copy(c).wait()
    out_copy.wait()


def exchange(nrow, ncol, exchange_ops, orbitals, potentials, chan, slot, pairs, coefs, basis):
    ndev = nrow * ncol
    terms, inner, width = exchange_ops.shape
    points = basis.shape[0]
    blocks = RBLK * BAND
    orb_rows = -(-orbitals.shape[0] // 8) * 8
    size = -(-max(ndev * CAP, 128) // 128) * 128
    span = -(-max(ndev * CAP, terms) // 128) * 128
    rest = inner - FIRST_ROWS
    any_spec = pl.BlockSpec(memory_space=pl.ANY)
    vmem = pl.BlockSpec(memory_space=pltpu.VMEM)
    dma = pltpu.SemaphoreType.DMA
    f32, bf16 = jnp.float32, jnp.bfloat16
    return pl.pallas_call(
        functools.partial(exchange_kernel, nrow, ncol),
        out_shape=(
            jax.ShapeDtypeStruct((ndev, CAP, inner, width), bf16),
            jax.ShapeDtypeStruct((blocks, width, width), bf16),
            jax.ShapeDtypeStruct((8, size), jnp.int32),
        ),
        in_specs=[any_spec] + [vmem] * 7,
        out_specs=(any_spec, any_spec, vmem),
        scratch_shapes=[
            pltpu.VMEM((terms, FIRST_ROWS, width), bf16),
            pltpu.VMEM((terms, rest, width), bf16),
            pltpu.VMEM((terms, max(rest, FIRST_ROWS), width), bf16),
            pltpu.VMEM((ndev, CAP, FIRST_ROWS, width), bf16),
            pltpu.VMEM((ndev, CAP, rest, width), bf16),
            pltpu.VMEM((orb_rows, points), f32),
            pltpu.VMEM((2 * orb_rows, points // 2), bf16),
            pltpu.VMEM((ncol, 2 * orb_rows, points // 2), bf16),
            pltpu.VMEM((ndev, 1, 128), f32),
            pltpu.VMEM((ndev, 1, 128), f32),
            pltpu.VMEM((128, points), f32),
            pltpu.VMEM((width, points), f32),
            pltpu.VMEM((128, points), f32),
            pltpu.VMEM((blocks, width, width), bf16),
            pltpu.VMEM((8, span), jnp.int32),
            pltpu.SMEM((8, span), jnp.int32),
            dma((ncol,)),
            dma((ncol,)),
            dma((ndev,)),
            dma((ndev,)),
            dma((2, ndev)),
            dma((2, ndev)),
            dma((6,)),
        ],
        compiler_params=pltpu.CompilerParams(
            collective_id=0, has_side_effects=True, vmem_limit_bytes=VMEM_BYTES
        ),
        name="exchange",
    )(exchange_ops, orbitals, potentials, chan, slot, pairs, coefs, basis)


def blocks_kernel(lists_smem, recv_ref, inner_ref, local_ref, out_ref, inner_t, sums, joined):
    step = pl.program_id(0)
    f32 = jnp.float32

    @pl.when(step == 0)
    def _():
        inner_t[...] = inner_ref[...].astype(f32).T.astype(jnp.bfloat16)

    for i in range(BLOCKS_STEP):
        head = lists_smem[0, step * BLOCKS_STEP + i]

        @pl.when(head < 0)
        def _():
            joined[i] = jnp.zeros(joined.shape[1:], joined.dtype)

        @pl.when(head >= 0)
        def _():
            follower = lists_smem[1, head]

            @pl.when(follower < 0)
            def _():
                joined[i] = recv_ref[head]

            @pl.when(follower >= 0)
            def _():
                sums[...] = recv_ref[head].astype(f32)

                def more(s):
                    sums[...] += recv_ref[s].astype(f32)
                    return lists_smem[1, s]

                lax.while_loop(lambda s: s >= 0, more, follower)
                joined[i] = sums[...].astype(joined.dtype)

    for i in range(BLOCKS_STEP):
        swapped = jnp.dot(inner_t[...], joined[i], preferred_element_type=f32)
        out_ref[i] = (swapped + local_ref[i].astype(f32)).astype(out_ref.dtype)


def make_blocks(lists, received, local, basis):
    slots, inner, width = received.shape
    blocks = local.shape[0]
    tiles = pl.BlockSpec((BLOCKS_STEP, width, width), lambda i, s: (i, 0, 0))
    return pl.pallas_call(
        blocks_kernel,
        grid_spec=pltpu.PrefetchScalarGridSpec(
            num_scalar_prefetch=1,
            grid=(blocks // BLOCKS_STEP,),
            in_specs=[
                pl.BlockSpec(received.shape, lambda i, s: (0, 0, 0)),
                pl.BlockSpec((inner, width), lambda i, s: (0, 0)),
                tiles,
            ],
            out_specs=tiles,
            scratch_shapes=[
                pltpu.VMEM((width, inner), jnp.bfloat16),
                pltpu.VMEM((inner, width), jnp.float32),
                pltpu.VMEM((BLOCKS_STEP, inner, width), jnp.bfloat16),
            ],
        ),
        out_shape=jax.ShapeDtypeStruct((blocks, width, width), jnp.bfloat16),
        compiler_params=pltpu.CompilerParams(
            dimension_semantics=("arbitrary",), vmem_limit_bytes=VMEM_BYTES
        ),
        name="make_blocks",
    )(lists, received, basis, local)


def on_device(basis, potentials, orbitals, chan_orbital, pair_list, slot_list, coefs, exchange_ops):
    nrow = lax.axis_size("prow")
    ncol = lax.axis_size("pcol")
    inner, width = exchange_ops.shape[1:]
    received, local, lists = exchange(
        nrow,
        ncol,
        exchange_ops,
        orbitals,
        potentials,
        chan_orbital[None, :],
        slot_list[None, :],
        pair_list.T,
        coefs.T,
        basis,
    )
    blocks = make_blocks(lists, received.reshape(-1, inner, width), local, basis)
    return blocks.reshape(RBLK, 1, BAND, 1, width, width)


def solution(mesh):
    placed = (
        P(),
        P(),
        P("pcol", None),
        P(),
        P(("prow", "pcol"), None),
        P(("prow", "pcol")),
        P(("prow", "pcol"), None),
        P(("prow", "pcol"), None, None),
    )
    return jax.shard_map(
        on_device,
        mesh=mesh,
        in_specs=placed,
        out_specs=P(None, "prow", None, "pcol", None, None),
        check_vma=False,
    )
```

```python
import functools

import jax
import jax.numpy as jnp
from jax import lax
from jax.experimental import pallas as pl
from jax.experimental.pallas import tpu as pltpu
from jax.sharding import PartitionSpec as P

CAP = 2
BAND = 2
RBLK = 32
BLOCKS_STEP = 8
FIRST_ROWS = 32
SPAN = 16
NEAR_BYTES = 8 * 1024 * 1024
EXCHANGE_BYTES = 48 * 1024 * 1024
BLOCKS_BYTES = 40 * 1024 * 1024
MESH = pl.DeviceIdType.MESH
EXACT = lax.Precision.HIGHEST
FAR = 1.0e6


def product(left, right, left_dim, right_dim, precision=None):
    return lax.dot_general(
        left,
        right,
        (((left_dim,), (right_dim,)), ((), ())),
        precision=precision,
        preferred_element_type=jnp.float32,
    )


def iota(shape, dim):
    return lax.broadcasted_iota(jnp.int32, shape, dim)


def masked(index, mask, count):
    flipped = 0
    for b in range(count.bit_length() - 1):
        bits = lax.div(index, 2**b) + lax.div(mask, 2**b)
        flipped = flipped + lax.rem(bits, 2) * 2**b
    return flipped


def turned(row):
    n = row.shape[1]
    same = iota((n, n), 0) == iota((n, n), 1)
    return jnp.sum(jnp.where(same, row, jnp.zeros_like(row)), axis=1, keepdims=True)


def slot_order(slot, slots, table):
    n = slot.shape[1]
    col = turned(slot)
    under, over = iota((n, n), 0), iota((n, n), 1)
    same = col == slot
    rank = jnp.sum(jnp.where((col < slot) | (same & (under < over)), 1, 0), axis=0, keepdims=True)
    place = turned(rank) == over
    before = jnp.sum(jnp.where(same & (over < under), 1, 0), axis=1, keepdims=True)
    order = jnp.sum(jnp.where(place, under, 0), axis=0, keepdims=True)
    keeps = jnp.sum(jnp.where(place, before, 0), axis=0, keepdims=True)
    upto = jnp.where(col <= iota((n, slots), 1), 1, 0)
    last = jnp.sum(upto, axis=0, keepdims=True) - 1
    table[...] = jnp.zeros_like(table)
    table[0:1, :n] = order
    table[1:2, :n] = keeps
    table[2:3, :slots] = last


def exchange_kernel(
    nrow,
    ncol,
    ops_ref,
    orb_ref,
    pot_ref,
    chan_ref,
    slot_ref,
    pair_ref,
    coef_ref,
    basis_ref,
    recv_ref,
    local_ref,
    lists_ref,
    terms_a,
    terms_b,
    running,
    send_a,
    send_b,
    orb_wide,
    orb_send,
    all_orb,
    msg_send,
    msg_recv,
    pot_pad,
    basis_t,
    weights,
    table,
    order_smem,
    orb_ssem,
    orb_rsem,
    m_ssem,
    m_rsem,
    e_ssem,
    e_rsem,
    own_sem,
):
    p = lax.axis_index("prow")
    q = lax.axis_index("pcol")
    ndev = nrow * ncol
    me = p * ncol + q
    f32 = jnp.float32
    bf16 = jnp.bfloat16
    slots = ndev * CAP
    blocks = RBLK * BAND
    terms = slot_ref.shape[1]
    chans = chan_ref.shape[1]
    groups = chans // ncol
    points = pot_ref.shape[1]
    orb_per = orb_ref.shape[0]
    orb_rows = orb_wide.shape[0]
    top = terms - 1
    chunks = ((terms_a, send_a, 0), (terms_b, send_b, FIRST_ROWS))

    def peer(t):
        low = lax.rem(t, ncol)
        mask = 0
        for b in range(ncol.bit_length() - 1):
            mask = mask * 2 + lax.rem(lax.div(low, 2**b), 2)
        return (
            masked(p, lax.rem(lax.div(t, ncol) + t, nrow), nrow),
            masked(q, mask, ncol),
        )

    def each(count, action):
        def body(t, c):
            action(t)
            return c

        lax.fori_loop(1, count, body, 0)

    def load(c):
        buffer, _, start = chunks[c]
        return pltpu.make_async_copy(
            ops_ref.at[:, pl.ds(start, buffer.shape[1]), :], buffer, own_sem.at[c]
        )

    def remote(source, target, sems, t, device):
        return pltpu.make_async_remote_copy(
            src_ref=source,
            dst_ref=target,
            send_sem=sems[0].at[t],
            recv_sem=sems[1].at[t],
            device_id=device,
            device_id_type=MESH,
        )

    def orb_copy(t):
        return remote(
            orb_send, all_orb.at[q], (orb_ssem, orb_rsem), t, (p, lax.rem(q + t, ncol))
        )

    def msg_copy(t):
        pp, qq = peer(t)
        return remote(
            msg_send.at[pp * ncol + qq], msg_recv.at[me], (m_ssem, m_rsem), t, (pp, qq)
        )

    def landing(c):
        _, send, start = chunks[c]
        return recv_ref.at[me, :, pl.ds(start, send.shape[2]), :]

    def exch_copy(c, t):
        pp, qq = peer(t)
        return remote(
            chunks[c][1].at[pp * ncol + qq],
            landing(c),
            (e_ssem.at[c], e_rsem.at[c]),
            t,
            (pp, qq),
        )

    def own_copy(c):
        return pltpu.make_async_copy(chunks[c][1].at[me], landing(c), own_sem.at[2 + c])

    load(0).start()
    load(1).start()
    barrier = pltpu.get_barrier_semaphore()
    each(
        ndev,
        lambda t: pl.semaphore_signal(barrier, inc=1, device_id=peer(t), device_id_type=MESH),
    )

    orb_wide[...] = jnp.zeros_like(orb_wide)
    orb_wide[:orb_per, :] = orb_ref[...].astype(f32)
    orb_send[...] = jnp.concatenate(
        [orb_wide[:, : points // 2], orb_wide[:, points // 2 :]], axis=0
    ).astype(bf16)

    slot = slot_ref[...]
    first, second, multipole = pair_ref[0:1, :], pair_ref[1:2, :], pair_ref[2:3, :]
    offset = (second // ncol - first // ncol + groups) % groups
    block = (first // nrow * BAND + offset).astype(f32)
    kind = iota((128, terms), 0)
    lane = iota((ndev, 128), 1)
    message = jnp.zeros((ndev, 128), f32)
    for c in range(CAP):
        base = SPAN * c
        parts = jnp.where(kind == multipole + base, coef_ref[0:1, :], 0.0)
        parts = jnp.where(kind == base + 8, coef_ref[1:2, :], parts)
        match = slot == iota((ndev, terms), 0) * CAP + c
        message += product(jnp.where(match, 1.0, 0.0), parts, 1, 1, EXACT)
        number = jnp.max(jnp.where(match, block, -1.0), axis=1, keepdims=True)
        message = jnp.where(lane == base + 9, number, message)
    msg_send[...] = message.reshape(ndev, 1, 128)

    slot_order(slot, slots, table)
    order_copy = pltpu.make_async_copy(table, order_smem, own_sem.at[4])
    order_copy.start()
    pl.semaphore_wait(barrier, ndev - 1)
    each(ncol, lambda t: orb_copy(t).start())
    each(ndev, lambda t: msg_copy(t).start())
    order_copy.wait()

    for c, (buffer, send, _) in enumerate(chunks):
        height, width = buffer.shape[1:]
        load(c).wait()

        def add(i, total):
            kept = jnp.where(order_smem[1, i] > 0, total, jnp.zeros_like(total))
            total = kept + buffer[jnp.clip(order_smem[0, i], 0, top)].astype(f32)
            running[i, :height, :] = total.astype(bf16)
            return total

        lax.fori_loop(0, terms, add, jnp.zeros((height, width), f32), unroll=4)

        def place(o, carried):
            for k in range(CAP):
                end = jnp.clip(order_smem[2, o * CAP + k], 0, top)
                send[o, k] = running[end, :height, :]
            return carried

        lax.fori_loop(0, ndev, place, 0)
        each(ndev, lambda t: exch_copy(c, t).start())
        own_copy(c).start()

    each(ncol, lambda t: orb_copy(t).wait())
    all_orb[q] = orb_send[...]
    each(ndev, lambda t: msg_copy(t).wait())
    msg_recv[me] = msg_send[me]

    wide = all_orb[...].astype(f32)
    orbs = jnp.concatenate(
        [
            wide[:, :orb_rows, :].reshape(ncol * orb_rows, points // 2),
            wide[:, orb_rows:, :].reshape(ncol * orb_rows, points // 2),
        ],
        axis=1,
    ).astype(bf16)
    chan_row = chan_ref[...]
    chan_place = chan_row // orb_per * orb_rows + chan_row % orb_per
    owns = jnp.where(iota((ncol * orb_rows, chans), 0) == chan_place, 1.0, 0.0).astype(bf16)
    number = iota((128, chans), 0)
    first_chan = number // BAND * nrow + p
    second_chan = (first_chan // ncol + number % BAND) % groups * ncol + q

    def orbital_of(chan):
        hot = jnp.where(iota((128, chans), 1) == chan, 1.0, 0.0).astype(bf16)
        return product(product(hot, owns, 1, 1).astype(bf16), orbs, 1, 0)

    received = msg_recv[...].reshape(ndev, 128)
    numbers = []
    sums = jnp.zeros((128, 128), f32)
    for c in range(CAP):
        base = SPAN * c
        ids = jnp.sum(jnp.where(lane == base + 9, received, 0.0), axis=1, keepdims=True)
        numbers.append(ids)
        hot = jnp.where(lane.astype(f32) == ids, 1.0, 0.0)
        inside = (lane >= base) & (lane < base + 9)
        sums += product(hot, jnp.where(inside, received, 0.0), 0, 0, EXACT)
    pot_pad[...] = jnp.zeros_like(pot_pad)
    for c in range(CAP):
        pot_pad[SPAN * c : SPAN * c + 8, :] = pot_ref[...]
    lanes = iota((128, 128), 1)
    factor = jnp.sum(jnp.where(lanes % SPAN == 8, sums, 0.0), axis=1, keepdims=True)
    weights[...] = product(sums, pot_pad[...], 1, 0, EXACT) + factor * (
        orbital_of(first_chan) * orbital_of(second_chan)
    )

    size = lists_ref.shape[1]
    source = iota((ndev, size), 0)
    spot = iota((ndev, size), 1)
    row = jnp.full((1, size), -1.0, f32)
    for c in range(CAP):
        row += jnp.sum(
            jnp.where(spot == source * CAP + c, numbers[c] + 1.0, 0.0), axis=0, keepdims=True
        )
    col = turned(row)
    under = iota((size, size), 0).astype(f32)
    over = iota((size, size), 1).astype(f32)
    heads = jnp.min(jnp.where(col == over, under, FAR), axis=0, keepdims=True)
    nexts = jnp.min(jnp.where((col == row) & (under > over), under, FAR), axis=0, keepdims=True)
    lists_ref[...] = jnp.zeros_like(lists_ref)
    lists_ref[0:1, :] = jnp.where(heads < FAR, heads, -1.0).astype(jnp.int32)
    lists_ref[1:2, :] = jnp.where(nexts < FAR, nexts, -1.0).astype(jnp.int32)

    basis_t[...] = basis_ref[...].astype(f32).T

    def form(t, carried):
        scaled = (basis_t[...] * weights[pl.ds(t, 1), :]).astype(bf16)
        local_ref[t] = jnp.dot(
            scaled, basis_ref[...], preferred_element_type=f32
        ).astype(bf16)
        return carried

    lax.fori_loop(0, blocks, form, 0)
    for c in range(len(chunks)):
        each(ndev, lambda t: exch_copy(c, t).wait())
        own_copy(c).wait()


def exchange(nrow, ncol, exchange_ops, orbitals, potentials, chan, slot, pairs, coefs, basis):
    ndev = nrow * ncol
    terms, inner, width = exchange_ops.shape
    points = basis.shape[0]
    blocks = RBLK * BAND
    orb_rows = -(-orbitals.shape[0] // 8) * 8
    size = -(-max(ndev * CAP, 128) // 128) * 128
    span = -(-max(ndev * CAP, terms) // 128) * 128
    rest = inner - FIRST_ROWS
    near = ndev * CAP * inner * width * 2 <= NEAR_BYTES
    place = pltpu.VMEM if near else jax.ShapeDtypeStruct
    any_spec = pl.BlockSpec(memory_space=pl.ANY)
    vmem = pl.BlockSpec(memory_space=pltpu.VMEM)
    dma = pltpu.SemaphoreType.DMA
    f32, bf16 = jnp.float32, jnp.bfloat16
    return pl.pallas_call(
        functools.partial(exchange_kernel, nrow, ncol),
        out_shape=(
            place((ndev, CAP, inner, width), bf16),
            pltpu.VMEM((blocks, width, width), bf16),
            pltpu.VMEM((8, size), jnp.int32),
        ),
        in_specs=[any_spec] + [vmem] * 7,
        out_specs=(vmem if near else any_spec, vmem, vmem),
        scratch_shapes=[
            pltpu.VMEM((terms, FIRST_ROWS, width), bf16),
            pltpu.VMEM((terms, rest, width), bf16),
            pltpu.VMEM((terms, max(rest, FIRST_ROWS), width), bf16),
            pltpu.VMEM((ndev, CAP, FIRST_ROWS, width), bf16),
            pltpu.VMEM((ndev, CAP, rest, width), bf16),
            pltpu.VMEM((orb_rows, points), f32),
            pltpu.VMEM((2 * orb_rows, points // 2), bf16),
            pltpu.VMEM((ncol, 2 * orb_rows, points // 2), bf16),
            pltpu.VMEM((ndev, 1, 128), f32),
            pltpu.VMEM((ndev, 1, 128), f32),
            pltpu.VMEM((128, points), f32),
            pltpu.VMEM((width, points), f32),
            pltpu.VMEM((128, points), f32),
            pltpu.VMEM((8, span), jnp.int32),
            pltpu.SMEM((8, span), jnp.int32),
            dma((ncol,)),
            dma((ncol,)),
            dma((ndev,)),
            dma((ndev,)),
            dma((2, ndev)),
            dma((2, ndev)),
            dma((5,)),
        ],
        compiler_params=pltpu.CompilerParams(
            collective_id=0, has_side_effects=True, vmem_limit_bytes=EXCHANGE_BYTES
        ),
        name="exchange",
    )(exchange_ops, orbitals, potentials, chan, slot, pairs, coefs, basis)


def blocks_kernel(
    lists_ref,
    recv_ref,
    basis_ref,
    local_ref,
    out_ref,
    lists_smem,
    inner_t,
    sums,
    joined,
    formed,
    sems,
    lists_sem,
):
    f32 = jnp.float32
    steps = local_ref.shape[0] // BLOCKS_STEP
    lists_copy = pltpu.make_async_copy(lists_ref, lists_smem, lists_sem)
    lists_copy.start()
    inner_t[...] = basis_ref[: recv_ref.shape[1], :].astype(f32).T.astype(jnp.bfloat16)

    def leave(step):
        span = pl.ds(step * BLOCKS_STEP, BLOCKS_STEP)
        return pltpu.make_async_copy(formed.at[span], out_ref.at[span], sems.at[step])

    def work(step, carried):
        longest = jnp.int32(-1)
        for i in range(BLOCKS_STEP):
            head = lists_smem[0, step * BLOCKS_STEP + i]
            follower = jnp.where(head < 0, -1, lists_smem[1, jnp.maximum(head, 0)])
            third = jnp.where(follower < 0, -1, lists_smem[1, jnp.maximum(follower, 0)])
            longest = jnp.maximum(longest, third)
            one = recv_ref[jnp.maximum(head, 0)].astype(f32)
            two = recv_ref[jnp.maximum(follower, 0)].astype(f32)
            nothing = jnp.zeros_like(one)
            joined[i] = (
                jnp.where(head < 0, nothing, one) + jnp.where(follower < 0, nothing, two)
            ).astype(joined.dtype)

        @pl.when(longest >= 0)
        def _():
            def rejoin(i, c):
                head = lists_smem[0, step * BLOCKS_STEP + i]
                follower = jnp.where(head < 0, -1, lists_smem[1, jnp.maximum(head, 0)])
                third = jnp.where(follower < 0, -1, lists_smem[1, jnp.maximum(follower, 0)])

                @pl.when(third >= 0)
                def _():
                    sums[...] = recv_ref[head].astype(f32) + recv_ref[follower].astype(f32)

                    def more(s):
                        sums[...] += recv_ref[s].astype(f32)
                        return lists_smem[1, s]

                    lax.while_loop(lambda s: s >= 0, more, third)
                    joined[i] = sums[...].astype(joined.dtype)

                return c

            lax.fori_loop(0, BLOCKS_STEP, rejoin, 0)

        for i in range(BLOCKS_STEP):
            t = step * BLOCKS_STEP + i
            swapped = jnp.dot(inner_t[...], joined[i], preferred_element_type=f32)
            formed[t] = (swapped + local_ref[t].astype(f32)).astype(formed.dtype)
        leave(step).start()
        return carried

    lists_copy.wait()
    lax.fori_loop(0, steps, work, 0)

    def finish(step, carried):
        leave(step).wait()
        return carried

    lax.fori_loop(0, steps, finish, 0)


def make_blocks(lists, received, local, basis):
    slots, inner, width = received.shape
    blocks = local.shape[0]
    vmem = pl.BlockSpec(memory_space=pltpu.VMEM)
    return pl.pallas_call(
        blocks_kernel,
        in_specs=[
            vmem,
            vmem,
            vmem,
            vmem,
        ],
        out_specs=pl.BlockSpec(memory_space=pl.ANY),
        scratch_shapes=[
            pltpu.SMEM(lists.shape, jnp.int32),
            pltpu.VMEM((width, inner), jnp.bfloat16),
            pltpu.VMEM((inner, width), jnp.float32),
            pltpu.VMEM((BLOCKS_STEP, inner, width), jnp.bfloat16),
            pltpu.VMEM((blocks, width, width), jnp.bfloat16),
            pltpu.SemaphoreType.DMA((blocks // BLOCKS_STEP,)),
            pltpu.SemaphoreType.DMA,
        ],
        out_shape=jax.ShapeDtypeStruct((blocks, width, width), jnp.bfloat16),
        compiler_params=pltpu.CompilerParams(vmem_limit_bytes=BLOCKS_BYTES),
        name="make_blocks",
    )(lists, received, basis, local)


def on_device(basis, potentials, orbitals, chan_orbital, pair_list, slot_list, coefs, exchange_ops):
    nrow = lax.axis_size("prow")
    ncol = lax.axis_size("pcol")
    inner, width = exchange_ops.shape[1:]
    received, local, lists = exchange(
        nrow,
        ncol,
        exchange_ops,
        orbitals,
        potentials,
        chan_orbital[None, :],
        slot_list[None, :],
        pair_list.T,
        coefs.T,
        basis,
    )
    blocks = make_blocks(lists, received.reshape(-1, inner, width), local, basis)
    return blocks.reshape(RBLK, 1, BAND, 1, width, width)


def solution(mesh):
    placed = (
        P(),
        P(),
        P("pcol", None),
        P(),
        P(("prow", "pcol"), None),
        P(("prow", "pcol")),
        P(("prow", "pcol"), None),
        P(("prow", "pcol"), None, None),
    )
    return jax.shard_map(
        on_device,
        mesh=mesh,
        in_specs=placed,
        out_specs=P(None, "prow", None, "pcol", None, None),
        check_vma=False,
    )
```

```python
import functools

import jax
import jax.numpy as jnp
from jax import lax
from jax.experimental import pallas as pl
from jax.experimental.pallas import tpu as pltpu
from jax.sharding import PartitionSpec as P

CAP = 2
BAND = 2
RBLK = 32
BLOCKS_STEP = 8
FIRST_ROWS = 16
SPAN = 16
NEAR_BYTES = 8 * 1024 * 1024
EXCHANGE_BYTES = 48 * 1024 * 1024
BLOCKS_BYTES = 40 * 1024 * 1024
MESH = pl.DeviceIdType.MESH
EXACT = lax.Precision.HIGHEST
FAR = 1.0e6


def product(left, right, left_dim, right_dim, precision=None):
    return lax.dot_general(
        left,
        right,
        (((left_dim,), (right_dim,)), ((), ())),
        precision=precision,
        preferred_element_type=jnp.float32,
    )


def iota(shape, dim):
    return lax.broadcasted_iota(jnp.int32, shape, dim)


def masked(index, mask, count):
    flipped = 0
    for b in range(count.bit_length() - 1):
        bits = lax.div(index, 2**b) + lax.div(mask, 2**b)
        flipped = flipped + lax.rem(bits, 2) * 2**b
    return flipped


def turned(row):
    n = row.shape[1]
    same = iota((n, n), 0) == iota((n, n), 1)
    return jnp.sum(jnp.where(same, row, jnp.zeros_like(row)), axis=1, keepdims=True)


def slot_order(slot, slots, table):
    n = slot.shape[1]
    col = turned(slot)
    under, over = iota((n, n), 0), iota((n, n), 1)
    same = col == slot
    rank = jnp.sum(jnp.where((col < slot) | (same & (under < over)), 1, 0), axis=0, keepdims=True)
    place = turned(rank) == over
    before = jnp.sum(jnp.where(same & (over < under), 1, 0), axis=1, keepdims=True)
    order = jnp.sum(jnp.where(place, under, 0), axis=0, keepdims=True)
    keeps = jnp.sum(jnp.where(place, before, 0), axis=0, keepdims=True)
    upto = jnp.where(col <= iota((n, slots), 1), 1, 0)
    last = jnp.sum(upto, axis=0, keepdims=True) - 1
    table[...] = jnp.zeros_like(table)
    table[0:1, :n] = order
    table[1:2, :n] = keeps
    table[2:3, :slots] = last


def exchange_kernel(
    nrow,
    ncol,
    ops_ref,
    orb_ref,
    pot_ref,
    chan_ref,
    slot_ref,
    pair_ref,
    coef_ref,
    basis_ref,
    recv_ref,
    local_ref,
    lists_ref,
    terms_a,
    terms_b,
    running,
    send_a,
    send_b,
    orb_wide,
    orb_send,
    all_orb,
    msg_send,
    msg_recv,
    pot_pad,
    basis_t,
    weights,
    table,
    order_smem,
    orb_ssem,
    orb_rsem,
    m_ssem,
    m_rsem,
    e_ssem,
    e_rsem,
    own_sem,
):
    p = lax.axis_index("prow")
    q = lax.axis_index("pcol")
    ndev = nrow * ncol
    me = p * ncol + q
    f32 = jnp.float32
    bf16 = jnp.bfloat16
    slots = ndev * CAP
    blocks = RBLK * BAND
    terms = slot_ref.shape[1]
    chans = chan_ref.shape[1]
    groups = chans // ncol
    points = pot_ref.shape[1]
    orb_per = orb_ref.shape[0]
    orb_rows = orb_wide.shape[0]
    top = terms - 1
    chunks = ((terms_a, send_a, 0), (terms_b, send_b, FIRST_ROWS))

    def peer(t):
        low = lax.rem(t, ncol)
        mask = 0
        for b in range(ncol.bit_length() - 1):
            mask = mask * 2 + lax.rem(lax.div(low, 2**b), 2)
        return (
            masked(p, lax.rem(lax.div(t, ncol) + t, nrow), nrow),
            masked(q, mask, ncol),
        )

    def each(count, action):
        def body(t, c):
            action(t)
            return c

        lax.fori_loop(1, count, body, 0)

    def load(c):
        buffer, _, start = chunks[c]
        return pltpu.make_async_copy(
            ops_ref.at[:, pl.ds(start, buffer.shape[1]), :], buffer, own_sem.at[c]
        )

    def remote(source, target, sems, t, device):
        return pltpu.make_async_remote_copy(
            src_ref=source,
            dst_ref=target,
            send_sem=sems[0].at[t],
            recv_sem=sems[1].at[t],
            device_id=device,
            device_id_type=MESH,
        )

    def orb_copy(t):
        return remote(
            orb_send, all_orb.at[q], (orb_ssem, orb_rsem), t, (p, lax.rem(q + t, ncol))
        )

    def msg_copy(t):
        pp, qq = peer(t)
        return remote(
            msg_send.at[pp * ncol + qq], msg_recv.at[me], (m_ssem, m_rsem), t, (pp, qq)
        )

    def landing(c):
        _, send, start = chunks[c]
        return recv_ref.at[me, :, pl.ds(start, send.shape[2]), :]

    def exch_copy(c, t):
        pp, qq = peer(t)
        return remote(
            chunks[c][1].at[pp * ncol + qq],
            landing(c),
            (e_ssem.at[c], e_rsem.at[c]),
            t,
            (pp, qq),
        )

    def own_copy(c):
        return pltpu.make_async_copy(chunks[c][1].at[me], landing(c), own_sem.at[2 + c])

    load(0).start()
    load(1).start()
    barrier = pltpu.get_barrier_semaphore()
    each(
        ndev,
        lambda t: pl.semaphore_signal(barrier, inc=1, device_id=peer(t), device_id_type=MESH),
    )

    slot = slot_ref[...]
    slot_order(slot, slots, table)
    order_copy = pltpu.make_async_copy(table, order_smem, own_sem.at[4])
    order_copy.start()
    order_copy.wait()

    def add_slots(c):
        buffer, send, _ = chunks[c]
        height, width = buffer.shape[1:]
        load(c).wait()

        def add(i, total):
            kept = jnp.where(order_smem[1, i] > 0, total, jnp.zeros_like(total))
            total = kept + buffer[jnp.clip(order_smem[0, i], 0, top)].astype(f32)
            running[i, :height, :] = total.astype(bf16)
            return total

        lax.fori_loop(0, terms, add, jnp.zeros((height, width), f32), unroll=4)

        def place(o, carried):
            for k in range(CAP):
                end = jnp.clip(order_smem[2, o * CAP + k], 0, top)
                send[o, k] = running[end, :height, :]
            return carried

        lax.fori_loop(0, ndev, place, 0)

    add_slots(0)
    pl.semaphore_wait(barrier, ndev - 1)
    each(ndev, lambda t: exch_copy(0, t).start())
    own_copy(0).start()

    orb_wide[...] = jnp.zeros_like(orb_wide)
    orb_wide[:orb_per, :] = orb_ref[...].astype(f32)
    orb_send[...] = jnp.concatenate(
        [orb_wide[:, : points // 2], orb_wide[:, points // 2 :]], axis=0
    ).astype(bf16)

    first, second, multipole = pair_ref[0:1, :], pair_ref[1:2, :], pair_ref[2:3, :]
    offset = (second // ncol - first // ncol + groups) % groups
    block = (first // nrow * BAND + offset).astype(f32)
    kind = iota((128, terms), 0)
    lane = iota((ndev, 128), 1)
    message = jnp.zeros((ndev, 128), f32)
    for c in range(CAP):
        base = SPAN * c
        parts = jnp.where(kind == multipole + base, coef_ref[0:1, :], 0.0)
        parts = jnp.where(kind == base + 8, coef_ref[1:2, :], parts)
        match = slot == iota((ndev, terms), 0) * CAP + c
        message += product(jnp.where(match, 1.0, 0.0), parts, 1, 1, EXACT)
        number = jnp.max(jnp.where(match, block, -1.0), axis=1, keepdims=True)
        message = jnp.where(lane == base + 9, number, message)
    msg_send[...] = message.reshape(ndev, 1, 128)

    each(ncol, lambda t: orb_copy(t).start())
    each(ndev, lambda t: msg_copy(t).start())

    add_slots(1)
    each(ndev, lambda t: exch_copy(1, t).start())
    own_copy(1).start()

    each(ncol, lambda t: orb_copy(t).wait())
    all_orb[q] = orb_send[...]
    each(ndev, lambda t: msg_copy(t).wait())
    msg_recv[me] = msg_send[me]

    wide = all_orb[...].astype(f32)
    orbs = jnp.concatenate(
        [
            wide[:, :orb_rows, :].reshape(ncol * orb_rows, points // 2),
            wide[:, orb_rows:, :].reshape(ncol * orb_rows, points // 2),
        ],
        axis=1,
    ).astype(bf16)
    chan_row = chan_ref[...]
    chan_place = chan_row // orb_per * orb_rows + chan_row % orb_per
    owns = jnp.where(iota((ncol * orb_rows, chans), 0) == chan_place, 1.0, 0.0).astype(bf16)
    number = iota((128, chans), 0)
    first_chan = number // BAND * nrow + p
    second_chan = (first_chan // ncol + number % BAND) % groups * ncol + q

    def orbital_of(chan):
        hot = jnp.where(iota((128, chans), 1) == chan, 1.0, 0.0).astype(bf16)
        return product(product(hot, owns, 1, 1).astype(bf16), orbs, 1, 0)

    received = msg_recv[...].reshape(ndev, 128)
    numbers = []
    sums = jnp.zeros((128, 128), f32)
    for c in range(CAP):
        base = SPAN * c
        ids = jnp.sum(jnp.where(lane == base + 9, received, 0.0), axis=1, keepdims=True)
        numbers.append(ids)
        hot = jnp.where(lane.astype(f32) == ids, 1.0, 0.0)
        inside = (lane >= base) & (lane < base + 9)
        sums += product(hot, jnp.where(inside, received, 0.0), 0, 0, EXACT)
    pot_pad[...] = jnp.zeros_like(pot_pad)
    for c in range(CAP):
        pot_pad[SPAN * c : SPAN * c + 8, :] = pot_ref[...]
    lanes = iota((128, 128), 1)
    factor = jnp.sum(jnp.where(lanes % SPAN == 8, sums, 0.0), axis=1, keepdims=True)
    weights[...] = product(sums, pot_pad[...], 1, 0, EXACT) + factor * (
        orbital_of(first_chan) * orbital_of(second_chan)
    )

    size = lists_ref.shape[1]
    source = iota((ndev, size), 0)
    spot = iota((ndev, size), 1)
    row = jnp.full((1, size), -1.0, f32)
    for c in range(CAP):
        row += jnp.sum(
            jnp.where(spot == source * CAP + c, numbers[c] + 1.0, 0.0), axis=0, keepdims=True
        )
    col = turned(row)
    under = iota((size, size), 0).astype(f32)
    over = iota((size, size), 1).astype(f32)
    heads = jnp.min(jnp.where(col == over, under, FAR), axis=0, keepdims=True)
    nexts = jnp.min(jnp.where((col == row) & (under > over), under, FAR), axis=0, keepdims=True)
    lists_ref[...] = jnp.zeros_like(lists_ref)
    lists_ref[0:1, :] = jnp.where(heads < FAR, heads, -1.0).astype(jnp.int32)
    lists_ref[1:2, :] = jnp.where(nexts < FAR, nexts, -1.0).astype(jnp.int32)

    basis_t[...] = basis_ref[...].astype(f32).T

    def form(t, carried):
        scaled = (basis_t[...] * weights[pl.ds(t, 1), :]).astype(bf16)
        local_ref[t] = jnp.dot(
            scaled, basis_ref[...], preferred_element_type=f32
        ).astype(bf16)
        return carried

    lax.fori_loop(0, blocks, form, 0)
    for c in range(len(chunks)):
        each(ndev, lambda t: exch_copy(c, t).wait())
        own_copy(c).wait()


def exchange(nrow, ncol, exchange_ops, orbitals, potentials, chan, slot, pairs, coefs, basis):
    ndev = nrow * ncol
    terms, inner, width = exchange_ops.shape
    points = basis.shape[0]
    blocks = RBLK * BAND
    orb_rows = -(-orbitals.shape[0] // 8) * 8
    size = -(-max(ndev * CAP, 128) // 128) * 128
    span = -(-max(ndev * CAP, terms) // 128) * 128
    rest = inner - FIRST_ROWS
    near = ndev * CAP * inner * width * 2 <= NEAR_BYTES
    place = pltpu.VMEM if near else jax.ShapeDtypeStruct
    any_spec = pl.BlockSpec(memory_space=pl.ANY)
    vmem = pl.BlockSpec(memory_space=pltpu.VMEM)
    dma = pltpu.SemaphoreType.DMA
    f32, bf16 = jnp.float32, jnp.bfloat16
    return pl.pallas_call(
        functools.partial(exchange_kernel, nrow, ncol),
        out_shape=(
            place((ndev, CAP, inner, width), bf16),
            pltpu.VMEM((blocks, width, width), bf16),
            jax.ShapeDtypeStruct((8, size), jnp.int32),
        ),
        in_specs=[any_spec] + [vmem] * 7,
        out_specs=(vmem if near else any_spec, vmem, vmem),
        scratch_shapes=[
            pltpu.VMEM((terms, FIRST_ROWS, width), bf16),
            pltpu.VMEM((terms, rest, width), bf16),
            pltpu.VMEM((terms, max(rest, FIRST_ROWS), width), bf16),
            pltpu.VMEM((ndev, CAP, FIRST_ROWS, width), bf16),
            pltpu.VMEM((ndev, CAP, rest, width), bf16),
            pltpu.VMEM((orb_rows, points), f32),
            pltpu.VMEM((2 * orb_rows, points // 2), bf16),
            pltpu.VMEM((ncol, 2 * orb_rows, points // 2), bf16),
            pltpu.VMEM((ndev, 1, 128), f32),
            pltpu.VMEM((ndev, 1, 128), f32),
            pltpu.VMEM((128, points), f32),
            pltpu.VMEM((width, points), f32),
            pltpu.VMEM((128, points), f32),
            pltpu.VMEM((8, span), jnp.int32),
            pltpu.SMEM((8, span), jnp.int32),
            dma((ncol,)),
            dma((ncol,)),
            dma((ndev,)),
            dma((ndev,)),
            dma((2, ndev)),
            dma((2, ndev)),
            dma((5,)),
        ],
        compiler_params=pltpu.CompilerParams(
            collective_id=0, has_side_effects=True, vmem_limit_bytes=EXCHANGE_BYTES
        ),
        name="exchange",
    )(exchange_ops, orbitals, potentials, chan, slot, pairs, coefs, basis)


def blocks_kernel(
    lists_ref,
    recv_ref,
    basis_ref,
    local_ref,
    out_ref,
    lists_smem,
    inner_t,
    sums,
    joined_a,
    joined_b,
    formed,
    sems,
    lists_sem,
):
    f32 = jnp.float32
    steps = local_ref.shape[0] // BLOCKS_STEP
    lists_copy = pltpu.make_async_copy(lists_ref, lists_smem, lists_sem)
    lists_copy.start()
    inner_t[...] = basis_ref[: recv_ref.shape[1], :].astype(f32).T.astype(jnp.bfloat16)

    def leave(step):
        span = pl.ds(step * BLOCKS_STEP, BLOCKS_STEP)
        return pltpu.make_async_copy(formed.at[span], out_ref.at[span], sems.at[step])

    def slots_of(step, i):
        head = lists_smem[0, step * BLOCKS_STEP + i]
        follower = jnp.where(head < 0, -1, lists_smem[1, jnp.maximum(head, 0)])
        third = jnp.where(follower < 0, -1, lists_smem[1, jnp.maximum(follower, 0)])
        return head, follower, third

    def join(step, joined, i):
        head, follower, third = slots_of(step, i)
        one = recv_ref[jnp.maximum(head, 0)].astype(f32)
        two = recv_ref[jnp.maximum(follower, 0)].astype(f32)
        nothing = jnp.zeros_like(one)
        joined[i] = (
            jnp.where(head < 0, nothing, one) + jnp.where(follower < 0, nothing, two)
        ).astype(joined.dtype)
        return third

    def multiply(step, joined, i):
        t = step * BLOCKS_STEP + i
        swapped = jnp.dot(inner_t[...], joined[i], preferred_element_type=f32)
        formed[t] = (swapped + local_ref[t].astype(f32)).astype(formed.dtype)

    def join_long(step, joined, longest):
        @pl.when(longest >= 0)
        def _():
            def rejoin(i, c):
                head, follower, third = slots_of(step, i)

                @pl.when(third >= 0)
                def _():
                    sums[...] = recv_ref[head].astype(f32) + recv_ref[follower].astype(f32)

                    def more(s):
                        sums[...] += recv_ref[s].astype(f32)
                        after = lists_smem[1, s]
                        return jnp.where(after > s, after, -1)

                    lax.while_loop(lambda s: s >= 0, more, third)
                    joined[i] = sums[...].astype(joined.dtype)

                return c

            lax.fori_loop(0, BLOCKS_STEP, rejoin, 0)

    def work(step, now, later):
        following = jnp.minimum(step + 1, steps - 1)
        longest = jnp.int32(-1)
        for i in range(BLOCKS_STEP):
            multiply(step, now, i)
            longest = jnp.maximum(longest, join(following, later, i))
        leave(step).start()
        join_long(following, later, longest)

    def work_pair(pair, carried):
        work(2 * pair, joined_a, joined_b)
        work(2 * pair + 1, joined_b, joined_a)
        return carried

    lists_copy.wait()
    longest = jnp.int32(-1)
    for i in range(BLOCKS_STEP):
        longest = jnp.maximum(longest, join(0, joined_a, i))
    join_long(0, joined_a, longest)
    lax.fori_loop(0, steps // 2, work_pair, 0)

    def finish(step, carried):
        leave(step).wait()
        return carried

    lax.fori_loop(0, steps, finish, 0)


def make_blocks(lists, received, local, basis):
    slots, inner, width = received.shape
    blocks = local.shape[0]
    vmem = pl.BlockSpec(memory_space=pltpu.VMEM)
    return pl.pallas_call(
        blocks_kernel,
        in_specs=[
            pl.BlockSpec(memory_space=pl.ANY),
            vmem,
            vmem,
            vmem,
        ],
        out_specs=pl.BlockSpec(memory_space=pl.ANY),
        scratch_shapes=[
            pltpu.SMEM(lists.shape, jnp.int32),
            pltpu.VMEM((width, inner), jnp.bfloat16),
            pltpu.VMEM((inner, width), jnp.float32),
            pltpu.VMEM((BLOCKS_STEP, inner, width), jnp.bfloat16),
            pltpu.VMEM((BLOCKS_STEP, inner, width), jnp.bfloat16),
            pltpu.VMEM((blocks, width, width), jnp.bfloat16),
            pltpu.SemaphoreType.DMA((blocks // BLOCKS_STEP,)),
            pltpu.SemaphoreType.DMA,
        ],
        out_shape=jax.ShapeDtypeStruct((blocks, width, width), jnp.bfloat16),
        compiler_params=pltpu.CompilerParams(vmem_limit_bytes=BLOCKS_BYTES),
        name="make_blocks",
    )(lists, received, basis, local)


def on_device(basis, potentials, orbitals, chan_orbital, pair_list, slot_list, coefs, exchange_ops):
    nrow = lax.axis_size("prow")
    ncol = lax.axis_size("pcol")
    inner, width = exchange_ops.shape[1:]
    received, local, lists = exchange(
        nrow,
        ncol,
        exchange_ops,
        orbitals,
        potentials,
        chan_orbital[None, :],
        slot_list[None, :],
        pair_list.T,
        coefs.T,
        basis,
    )
    blocks = make_blocks(lists, received.reshape(-1, inner, width), local, basis)
    return blocks.reshape(RBLK, 1, BAND, 1, width, width)


def solution(mesh):
    placed = (
        P(),
        P(),
        P("pcol", None),
        P(),
        P(("prow", "pcol"), None),
        P(("prow", "pcol")),
        P(("prow", "pcol"), None),
        P(("prow", "pcol"), None, None),
    )
    return jax.shard_map(
        on_device,
        mesh=mesh,
        in_specs=placed,
        out_specs=P(None, "prow", None, "pcol", None, None),
        check_vma=False,
    )
```

```python
import functools

import jax
import jax.numpy as jnp
from jax import lax
from jax.experimental import pallas as pl
from jax.experimental.pallas import tpu as pltpu
from jax.sharding import PartitionSpec as P

CAP = 2
BAND = 2
RBLK = 32
BLOCKS_STEP = 8
BANDS = (16, 32)
SPAN = 16
NEAR_BYTES = 8 * 1024 * 1024
EXCHANGE_BYTES = 48 * 1024 * 1024
BLOCKS_BYTES = 40 * 1024 * 1024
MESH = pl.DeviceIdType.MESH
EXACT = lax.Precision.HIGHEST
FAR = 1.0e6


def product(left, right, left_dim, right_dim, precision=None):
    return lax.dot_general(
        left,
        right,
        (((left_dim,), (right_dim,)), ((), ())),
        precision=precision,
        preferred_element_type=jnp.float32,
    )


def iota(shape, dim):
    return lax.broadcasted_iota(jnp.int32, shape, dim)


def masked(index, mask, count):
    flipped = 0
    for b in range(count.bit_length() - 1):
        bits = lax.div(index, 2**b) + lax.div(mask, 2**b)
        flipped = flipped + lax.rem(bits, 2) * 2**b
    return flipped


def turned(row):
    n = row.shape[1]
    same = iota((n, n), 0) == iota((n, n), 1)
    return jnp.sum(jnp.where(same, row, jnp.zeros_like(row)), axis=1, keepdims=True)


def slot_order(slot, slots, table):
    n = slot.shape[1]
    col = turned(slot)
    under, over = iota((n, n), 0), iota((n, n), 1)
    same = col == slot
    rank = jnp.sum(jnp.where((col < slot) | (same & (under < over)), 1, 0), axis=0, keepdims=True)
    place = turned(rank) == over
    before = jnp.sum(jnp.where(same & (over < under), 1, 0), axis=1, keepdims=True)
    order = jnp.sum(jnp.where(place, under, 0), axis=0, keepdims=True)
    keeps = jnp.sum(jnp.where(place, before, 0), axis=0, keepdims=True)
    upto = jnp.where(col <= iota((n, slots), 1), 1, 0)
    last = jnp.sum(upto, axis=0, keepdims=True) - 1
    table[...] = jnp.zeros_like(table)
    table[0:1, :n] = order
    table[1:2, :n] = keeps
    table[2:3, :slots] = last


def exchange_kernel(
    nrow,
    ncol,
    ops_ref,
    orb_ref,
    pot_ref,
    chan_ref,
    slot_ref,
    pair_ref,
    coef_ref,
    basis_ref,
    recv_ref,
    local_ref,
    lists_ref,
    terms_a,
    terms_b,
    terms_c,
    running,
    send_a,
    send_b,
    send_c,
    lists,
    orb_wide,
    orb_send,
    all_orb,
    msg_send,
    msg_recv,
    pot_pad,
    basis_t,
    weights,
    table,
    order_smem,
    orb_ssem,
    orb_rsem,
    m_ssem,
    m_rsem,
    e_ssem,
    e_rsem,
    own_sem,
):
    p = lax.axis_index("prow")
    q = lax.axis_index("pcol")
    ndev = nrow * ncol
    me = p * ncol + q
    f32 = jnp.float32
    bf16 = jnp.bfloat16
    slots = ndev * CAP
    blocks = RBLK * BAND
    terms = slot_ref.shape[1]
    chans = chan_ref.shape[1]
    groups = chans // ncol
    points = pot_ref.shape[1]
    orb_per = orb_ref.shape[0]
    orb_rows = orb_wide.shape[0]
    top = terms - 1
    chunks = (
        (terms_a, send_a, 0),
        (terms_b, send_b, BANDS[0]),
        (terms_c, send_c, BANDS[0] + BANDS[1]),
    )

    def peer(t):
        low = lax.rem(t, ncol)
        mask = 0
        for b in range(ncol.bit_length() - 1):
            mask = mask * 2 + lax.rem(lax.div(low, 2**b), 2)
        return (
            masked(p, lax.rem(lax.div(t, ncol) + t, nrow), nrow),
            masked(q, mask, ncol),
        )

    def each(count, action):
        def body(t, c):
            action(t)
            return c

        lax.fori_loop(1, count, body, 0)

    def load(c):
        buffer, _, start = chunks[c]
        return pltpu.make_async_copy(
            ops_ref.at[:, pl.ds(start, buffer.shape[1]), :], buffer, own_sem.at[c]
        )

    def remote(source, target, sems, t, device):
        return pltpu.make_async_remote_copy(
            src_ref=source,
            dst_ref=target,
            send_sem=sems[0].at[t],
            recv_sem=sems[1].at[t],
            device_id=device,
            device_id_type=MESH,
        )

    def orb_copy(t):
        return remote(
            orb_send, all_orb.at[q], (orb_ssem, orb_rsem), t, (p, lax.rem(q + t, ncol))
        )

    def msg_copy(t):
        pp, qq = peer(t)
        return remote(
            msg_send.at[pp * ncol + qq], msg_recv.at[me], (m_ssem, m_rsem), t, (pp, qq)
        )

    def landing(c):
        _, send, start = chunks[c]
        return recv_ref.at[me, :, pl.ds(start, send.shape[2]), :]

    def exch_copy(c, t):
        pp, qq = peer(t)
        return remote(
            chunks[c][1].at[pp * ncol + qq],
            landing(c),
            (e_ssem.at[c], e_rsem.at[c]),
            t,
            (pp, qq),
        )

    def own_copy(c):
        return pltpu.make_async_copy(chunks[c][1].at[me], landing(c), own_sem.at[3 + c])

    for c in range(len(chunks)):
        load(c).start()
    barrier = pltpu.get_barrier_semaphore()
    each(
        ndev,
        lambda t: pl.semaphore_signal(barrier, inc=1, device_id=peer(t), device_id_type=MESH),
    )

    slot = slot_ref[...]
    slot_order(slot, slots, table)
    order_copy = pltpu.make_async_copy(table, order_smem, own_sem.at[6])
    order_copy.start()
    order_copy.wait()

    def add_slots(c):
        buffer, send, _ = chunks[c]
        height, width = buffer.shape[1:]
        load(c).wait()

        def add(i, total):
            kept = jnp.where(order_smem[1, i] > 0, total, jnp.zeros_like(total))
            total = kept + buffer[jnp.clip(order_smem[0, i], 0, top)].astype(f32)
            running[i, :height, :] = total.astype(bf16)
            return total

        lax.fori_loop(0, terms, add, jnp.zeros((height, width), f32), unroll=4)

        def place(o, carried):
            for k in range(CAP):
                end = jnp.clip(order_smem[2, o * CAP + k], 0, top)
                send[o, k] = running[end, :height, :]
            return carried

        lax.fori_loop(0, ndev, place, 0)

    add_slots(0)
    pl.semaphore_wait(barrier, ndev - 1)
    each(ndev, lambda t: exch_copy(0, t).start())
    own_copy(0).start()

    orb_wide[...] = jnp.zeros_like(orb_wide)
    orb_wide[:orb_per, :] = orb_ref[...].astype(f32)
    orb_send[...] = jnp.concatenate(
        [orb_wide[:, : points // 2], orb_wide[:, points // 2 :]], axis=0
    ).astype(bf16)

    first, second, multipole = pair_ref[0:1, :], pair_ref[1:2, :], pair_ref[2:3, :]
    offset = (second // ncol - first // ncol + groups) % groups
    block = (first // nrow * BAND + offset).astype(f32)
    kind = iota((128, terms), 0)
    lane = iota((ndev, 128), 1)
    message = jnp.zeros((ndev, 128), f32)
    for c in range(CAP):
        base = SPAN * c
        parts = jnp.where(kind == multipole + base, coef_ref[0:1, :], 0.0)
        parts = jnp.where(kind == base + 8, coef_ref[1:2, :], parts)
        match = slot == iota((ndev, terms), 0) * CAP + c
        message += product(jnp.where(match, 1.0, 0.0), parts, 1, 1, EXACT)
        number = jnp.max(jnp.where(match, block, -1.0), axis=1, keepdims=True)
        message = jnp.where(lane == base + 9, number, message)
    msg_send[...] = message.reshape(ndev, 1, 128)

    each(ncol, lambda t: orb_copy(t).start())
    each(ndev, lambda t: msg_copy(t).start())

    for c in range(1, len(chunks)):
        add_slots(c)
        each(ndev, lambda t: exch_copy(c, t).start())
        own_copy(c).start()

    each(ncol, lambda t: orb_copy(t).wait())
    all_orb[q] = orb_send[...]
    each(ndev, lambda t: msg_copy(t).wait())
    msg_recv[me] = msg_send[me]

    wide = all_orb[...].astype(f32)
    orbs = jnp.concatenate(
        [
            wide[:, :orb_rows, :].reshape(ncol * orb_rows, points // 2),
            wide[:, orb_rows:, :].reshape(ncol * orb_rows, points // 2),
        ],
        axis=1,
    ).astype(bf16)
    chan_row = chan_ref[...]
    chan_place = chan_row // orb_per * orb_rows + chan_row % orb_per
    owns = jnp.where(iota((ncol * orb_rows, chans), 0) == chan_place, 1.0, 0.0).astype(bf16)
    number = iota((128, chans), 0)
    first_chan = number // BAND * nrow + p
    second_chan = (first_chan // ncol + number % BAND) % groups * ncol + q

    def orbital_of(chan):
        hot = jnp.where(iota((128, chans), 1) == chan, 1.0, 0.0).astype(bf16)
        return product(product(hot, owns, 1, 1).astype(bf16), orbs, 1, 0)

    received = msg_recv[...].reshape(ndev, 128)
    numbers = []
    sums = jnp.zeros((128, 128), f32)
    for c in range(CAP):
        base = SPAN * c
        ids = jnp.sum(jnp.where(lane == base + 9, received, 0.0), axis=1, keepdims=True)
        numbers.append(ids)
        hot = jnp.where(lane.astype(f32) == ids, 1.0, 0.0)
        inside = (lane >= base) & (lane < base + 9)
        sums += product(hot, jnp.where(inside, received, 0.0), 0, 0, EXACT)
    pot_pad[...] = jnp.zeros_like(pot_pad)
    for c in range(CAP):
        pot_pad[SPAN * c : SPAN * c + 8, :] = pot_ref[...]
    lanes = iota((128, 128), 1)
    factor = jnp.sum(jnp.where(lanes % SPAN == 8, sums, 0.0), axis=1, keepdims=True)
    weights[...] = product(sums, pot_pad[...], 1, 0, EXACT) + factor * (
        orbital_of(first_chan) * orbital_of(second_chan)
    )

    size = lists.shape[1]
    source = iota((ndev, size), 0)
    spot = iota((ndev, size), 1)
    row = jnp.full((1, size), -1.0, f32)
    for c in range(CAP):
        row += jnp.sum(
            jnp.where(spot == source * CAP + c, numbers[c] + 1.0, 0.0), axis=0, keepdims=True
        )
    col = turned(row)
    under = iota((size, size), 0).astype(f32)
    over = iota((size, size), 1).astype(f32)
    heads = jnp.min(jnp.where(col == over, under, FAR), axis=0, keepdims=True)
    nexts = jnp.min(jnp.where((col == row) & (under > over), under, FAR), axis=0, keepdims=True)
    lists[...] = jnp.zeros_like(lists)
    lists[0:1, :] = jnp.where(heads < FAR, heads, -1.0).astype(jnp.int32)
    lists[1:2, :] = jnp.where(nexts < FAR, nexts, -1.0).astype(jnp.int32)

    lists_copy = pltpu.make_async_copy(lists, lists_ref, own_sem.at[7])
    lists_copy.start()
    basis_t[...] = basis_ref[...].astype(f32).T

    def form(t, carried):
        scaled = (basis_t[...] * weights[pl.ds(t, 1), :]).astype(bf16)
        local_ref[t] = jnp.dot(
            scaled, basis_ref[...], preferred_element_type=f32
        ).astype(bf16)
        return carried

    lax.fori_loop(0, blocks, form, 0)
    for c in range(len(chunks)):
        each(ndev, lambda t: exch_copy(c, t).wait())
        own_copy(c).wait()
    lists_copy.wait()


def exchange(nrow, ncol, exchange_ops, orbitals, potentials, chan, slot, pairs, coefs, basis):
    ndev = nrow * ncol
    terms, inner, width = exchange_ops.shape
    points = basis.shape[0]
    blocks = RBLK * BAND
    orb_rows = -(-orbitals.shape[0] // 8) * 8
    size = -(-max(ndev * CAP, 128) // 128) * 128
    span = -(-max(ndev * CAP, terms) // 128) * 128
    heights = BANDS + (inner - sum(BANDS),)
    near = ndev * CAP * inner * width * 2 <= NEAR_BYTES
    place = pltpu.VMEM if near else jax.ShapeDtypeStruct
    any_spec = pl.BlockSpec(memory_space=pl.ANY)
    smem = pl.BlockSpec(memory_space=pltpu.SMEM)
    vmem = pl.BlockSpec(memory_space=pltpu.VMEM)
    dma = pltpu.SemaphoreType.DMA
    f32, bf16 = jnp.float32, jnp.bfloat16
    return pl.pallas_call(
        functools.partial(exchange_kernel, nrow, ncol),
        out_shape=(
            place((ndev, CAP, inner, width), bf16),
            pltpu.VMEM((blocks, width, width), bf16),
            pltpu.SMEM((8, size), jnp.int32),
        ),
        in_specs=[any_spec] + [vmem] * 7,
        out_specs=(vmem if near else any_spec, vmem, smem),
        scratch_shapes=[
            *[pltpu.VMEM((terms, rows, width), bf16) for rows in heights],
            pltpu.VMEM((terms, max(heights), width), bf16),
            *[pltpu.VMEM((ndev, CAP, rows, width), bf16) for rows in heights],
            pltpu.VMEM((8, size), jnp.int32),
            pltpu.VMEM((orb_rows, points), f32),
            pltpu.VMEM((2 * orb_rows, points // 2), bf16),
            pltpu.VMEM((ncol, 2 * orb_rows, points // 2), bf16),
            pltpu.VMEM((ndev, 1, 128), f32),
            pltpu.VMEM((ndev, 1, 128), f32),
            pltpu.VMEM((128, points), f32),
            pltpu.VMEM((width, points), f32),
            pltpu.VMEM((128, points), f32),
            pltpu.VMEM((8, span), jnp.int32),
            pltpu.SMEM((8, span), jnp.int32),
            dma((ncol,)),
            dma((ncol,)),
            dma((ndev,)),
            dma((ndev,)),
            dma((3, ndev)),
            dma((3, ndev)),
            dma((8,)),
        ],
        compiler_params=pltpu.CompilerParams(
            collective_id=0, has_side_effects=True, vmem_limit_bytes=EXCHANGE_BYTES
        ),
        name="exchange",
    )(exchange_ops, orbitals, potentials, chan, slot, pairs, coefs, basis)


def blocks_kernel(
    lists_smem,
    recv_ref,
    basis_ref,
    local_ref,
    out_ref,
    inner_t,
    sums,
    joined_a,
    joined_b,
    formed,
    sems,
):
    f32 = jnp.float32
    steps = local_ref.shape[0] // BLOCKS_STEP
    inner_t[...] = basis_ref[: recv_ref.shape[1], :].astype(f32).T.astype(jnp.bfloat16)

    def leave(step):
        span = pl.ds(step * BLOCKS_STEP, BLOCKS_STEP)
        return pltpu.make_async_copy(formed.at[span], out_ref.at[span], sems.at[step])

    def slots_of(step, i):
        head = lists_smem[0, step * BLOCKS_STEP + i]
        follower = jnp.where(head < 0, -1, lists_smem[1, jnp.maximum(head, 0)])
        third = jnp.where(follower < 0, -1, lists_smem[1, jnp.maximum(follower, 0)])
        return head, follower, third

    def join(step, joined, i):
        head, follower, third = slots_of(step, i)
        one = recv_ref[jnp.maximum(head, 0)]
        two = recv_ref[jnp.maximum(follower, 0)]
        nothing = jnp.zeros_like(one)
        joined[i] = jnp.where(head < 0, nothing, one) + jnp.where(follower < 0, nothing, two)
        return third

    def multiply(step, joined, i):
        t = step * BLOCKS_STEP + i
        swapped = jnp.dot(inner_t[...], joined[i], preferred_element_type=f32)
        formed[t] = (swapped + local_ref[t].astype(f32)).astype(formed.dtype)

    def join_long(step, joined, longest):
        @pl.when(longest >= 0)
        def _():
            def rejoin(i, c):
                head, follower, third = slots_of(step, i)

                @pl.when(third >= 0)
                def _():
                    sums[...] = recv_ref[head].astype(f32) + recv_ref[follower].astype(f32)

                    def more(s):
                        sums[...] += recv_ref[s].astype(f32)
                        after = lists_smem[1, s]
                        return jnp.where(after > s, after, -1)

                    lax.while_loop(lambda s: s >= 0, more, third)
                    joined[i] = sums[...].astype(joined.dtype)

                return c

            lax.fori_loop(0, BLOCKS_STEP, rejoin, 0)

    def work(step, now, later):
        following = jnp.minimum(step + 1, steps - 1)
        longest = jnp.int32(-1)
        for i in range(BLOCKS_STEP):
            multiply(step, now, i)
            longest = jnp.maximum(longest, join(following, later, i))
        leave(step).start()
        join_long(following, later, longest)

    def work_pair(pair, carried):
        work(2 * pair, joined_a, joined_b)
        work(2 * pair + 1, joined_b, joined_a)
        return carried

    longest = jnp.int32(-1)
    for i in range(BLOCKS_STEP):
        longest = jnp.maximum(longest, join(0, joined_a, i))
    join_long(0, joined_a, longest)
    lax.fori_loop(0, steps // 2, work_pair, 0)

    def finish(step, carried):
        leave(step).wait()
        return carried

    lax.fori_loop(0, steps, finish, 0)


def make_blocks(lists, received, local, basis):
    slots, inner, width = received.shape
    blocks = local.shape[0]
    vmem = pl.BlockSpec(memory_space=pltpu.VMEM)
    return pl.pallas_call(
        blocks_kernel,
        in_specs=[
            pl.BlockSpec(memory_space=pltpu.SMEM),
            vmem,
            vmem,
            vmem,
        ],
        out_specs=pl.BlockSpec(memory_space=pl.ANY),
        scratch_shapes=[
            pltpu.VMEM((width, inner), jnp.bfloat16),
            pltpu.VMEM((inner, width), jnp.float32),
            pltpu.VMEM((BLOCKS_STEP, inner, width), jnp.bfloat16),
            pltpu.VMEM((BLOCKS_STEP, inner, width), jnp.bfloat16),
            pltpu.VMEM((blocks, width, width), jnp.bfloat16),
            pltpu.SemaphoreType.DMA((blocks // BLOCKS_STEP,)),
        ],
        out_shape=jax.ShapeDtypeStruct((blocks, width, width), jnp.bfloat16),
        compiler_params=pltpu.CompilerParams(vmem_limit_bytes=BLOCKS_BYTES),
        name="make_blocks",
    )(lists, received, basis, local)


def on_device(basis, potentials, orbitals, chan_orbital, pair_list, slot_list, coefs, exchange_ops):
    nrow = lax.axis_size("prow")
    ncol = lax.axis_size("pcol")
    inner, width = exchange_ops.shape[1:]
    received, local, lists = exchange(
        nrow,
        ncol,
        exchange_ops,
        orbitals,
        potentials,
        chan_orbital[None, :],
        slot_list[None, :],
        pair_list.T,
        coefs.T,
        basis,
    )
    blocks = make_blocks(lists, received.reshape(-1, inner, width), local, basis)
    return blocks.reshape(RBLK, 1, BAND, 1, width, width)


def solution(mesh):
    placed = (
        P(),
        P(),
        P("pcol", None),
        P(),
        P(("prow", "pcol"), None),
        P(("prow", "pcol")),
        P(("prow", "pcol"), None),
        P(("prow", "pcol"), None, None),
    )
    return jax.shard_map(
        on_device,
        mesh=mesh,
        in_specs=placed,
        out_specs=P(None, "prow", None, "pcol", None, None),
        check_vma=False,
    )
```

```python
import functools

import jax
import jax.numpy as jnp
from jax import lax
from jax.experimental import pallas as pl
from jax.experimental.pallas import tpu as pltpu
from jax.sharding import PartitionSpec as P

CAP = 2
BAND = 2
RBLK = 32
BLOCKS_STEP = 8
BANDS = (16, 32)
SPAN = 16
NEAR_BYTES = 8 * 1024 * 1024
EXCHANGE_BYTES = 48 * 1024 * 1024
BLOCKS_BYTES = 40 * 1024 * 1024
MESH = pl.DeviceIdType.MESH
EXACT = lax.Precision.HIGHEST
FAR = 1.0e6


def product(left, right, left_dim, right_dim, precision=None):
    return lax.dot_general(
        left,
        right,
        (((left_dim,), (right_dim,)), ((), ())),
        precision=precision,
        preferred_element_type=jnp.float32,
    )


def iota(shape, dim):
    return lax.broadcasted_iota(jnp.int32, shape, dim)


def masked(index, mask, count):
    flipped = 0
    for b in range(count.bit_length() - 1):
        bits = lax.div(index, 2**b) + lax.div(mask, 2**b)
        flipped = flipped + lax.rem(bits, 2) * 2**b
    return flipped


def turned(row):
    n = row.shape[1]
    same = iota((n, n), 0) == iota((n, n), 1)
    return jnp.sum(jnp.where(same, row, jnp.zeros_like(row)), axis=1, keepdims=True)


def slot_order(slot, slots, table):
    n = slot.shape[1]
    col = turned(slot)
    under, over = iota((n, n), 0), iota((n, n), 1)
    same = col == slot
    rank = jnp.sum(jnp.where((col < slot) | (same & (under < over)), 1, 0), axis=0, keepdims=True)
    place = turned(rank) == over
    before = jnp.sum(jnp.where(same & (over < under), 1, 0), axis=1, keepdims=True)
    order = jnp.sum(jnp.where(place, under, 0), axis=0, keepdims=True)
    keeps = jnp.sum(jnp.where(place, before, 0), axis=0, keepdims=True)
    upto = jnp.where(col <= iota((n, slots), 1), 1, 0)
    last = jnp.sum(upto, axis=0, keepdims=True) - 1
    table[...] = jnp.zeros_like(table)
    table[0:1, :n] = order
    table[1:2, :n] = keeps
    table[2:3, :slots] = last


def exchange_kernel(
    nrow,
    ncol,
    ops_ref,
    orb_ref,
    pot_ref,
    chan_ref,
    slot_ref,
    pair_ref,
    coef_ref,
    basis_ref,
    recv_ref,
    local_ref,
    lists_ref,
    terms_a,
    terms_b,
    terms_c,
    running,
    send_a,
    send_b,
    send_c,
    lists,
    orb_wide,
    orb_send,
    all_orb,
    msg_send,
    msg_recv,
    pot_pad,
    basis_t,
    weights,
    table,
    order_smem,
    orb_ssem,
    orb_rsem,
    m_ssem,
    m_rsem,
    e_ssem,
    e_rsem,
    own_sem,
):
    p = lax.axis_index("prow")
    q = lax.axis_index("pcol")
    ndev = nrow * ncol
    me = p * ncol + q
    f32 = jnp.float32
    bf16 = jnp.bfloat16
    slots = ndev * CAP
    blocks = RBLK * BAND
    terms = slot_ref.shape[1]
    chans = chan_ref.shape[1]
    groups = chans // ncol
    points = pot_ref.shape[1]
    orb_per = orb_ref.shape[0]
    orb_rows = orb_wide.shape[0]
    top = terms - 1
    chunks = (
        (terms_a, send_a, 0),
        (terms_b, send_b, BANDS[0]),
        (terms_c, send_c, BANDS[0] + BANDS[1]),
    )

    def peer(t):
        left = ndev - t
        high = lax.div(left, nrow)
        return (
            masked(p, lax.rem(left + high, nrow), nrow),
            masked(q, lax.rem(high, ncol), ncol),
        )

    def each(count, action):
        def body(t, c):
            action(t)
            return c

        lax.fori_loop(1, count, body, 0)

    def load(c):
        buffer, _, start = chunks[c]
        return pltpu.make_async_copy(
            ops_ref.at[:, pl.ds(start, buffer.shape[1]), :], buffer, own_sem.at[c]
        )

    def remote(source, target, sems, t, device):
        return pltpu.make_async_remote_copy(
            src_ref=source,
            dst_ref=target,
            send_sem=sems[0].at[t],
            recv_sem=sems[1].at[t],
            device_id=device,
            device_id_type=MESH,
        )

    def orb_copy(t):
        return remote(
            orb_send, all_orb.at[q], (orb_ssem, orb_rsem), t, (p, lax.rem(q + t, ncol))
        )

    def msg_copy(t):
        pp, qq = peer(t)
        return remote(
            msg_send.at[pp * ncol + qq], msg_recv.at[me], (m_ssem, m_rsem), t, (pp, qq)
        )

    def landing(c):
        _, send, start = chunks[c]
        return recv_ref.at[me, :, pl.ds(start, send.shape[2]), :]

    def exch_copy(c, t):
        pp, qq = peer(t)
        return remote(
            chunks[c][1].at[pp * ncol + qq],
            landing(c),
            (e_ssem.at[c], e_rsem.at[c]),
            t,
            (pp, qq),
        )

    def own_copy(c):
        return pltpu.make_async_copy(chunks[c][1].at[me], landing(c), own_sem.at[3 + c])

    for c in range(len(chunks)):
        load(c).start()
    barrier = pltpu.get_barrier_semaphore()
    each(
        ndev,
        lambda t: pl.semaphore_signal(barrier, inc=1, device_id=peer(t), device_id_type=MESH),
    )

    slot = slot_ref[...]
    slot_order(slot, slots, table)
    order_copy = pltpu.make_async_copy(table, order_smem, own_sem.at[6])
    order_copy.start()
    order_copy.wait()

    def add_slots(c):
        buffer, send, _ = chunks[c]
        height, width = buffer.shape[1:]
        load(c).wait()

        def add(i, total):
            kept = jnp.where(order_smem[1, i] > 0, total, jnp.zeros_like(total))
            total = kept + buffer[jnp.clip(order_smem[0, i], 0, top)].astype(f32)
            running[i, :height, :] = total.astype(bf16)
            return total

        lax.fori_loop(0, terms, add, jnp.zeros((height, width), f32), unroll=4)

        def place(o, carried):
            for k in range(CAP):
                end = jnp.clip(order_smem[2, o * CAP + k], 0, top)
                send[o, k] = running[end, :height, :]
            return carried

        lax.fori_loop(0, ndev, place, 0)

    add_slots(0)
    pl.semaphore_wait(barrier, ndev - 1)
    each(ndev, lambda t: exch_copy(0, t).start())
    own_copy(0).start()

    orb_wide[...] = jnp.zeros_like(orb_wide)
    orb_wide[:orb_per, :] = orb_ref[...].astype(f32)
    orb_send[...] = jnp.concatenate(
        [orb_wide[:, : points // 2], orb_wide[:, points // 2 :]], axis=0
    ).astype(bf16)

    first, second, multipole = pair_ref[0:1, :], pair_ref[1:2, :], pair_ref[2:3, :]
    offset = (second // ncol - first // ncol + groups) % groups
    block = (first // nrow * BAND + offset).astype(f32)
    kind = iota((128, terms), 0)
    lane = iota((ndev, 128), 1)
    message = jnp.zeros((ndev, 128), f32)
    for c in range(CAP):
        base = SPAN * c
        parts = jnp.where(kind == multipole + base, coef_ref[0:1, :], 0.0)
        parts = jnp.where(kind == base + 8, coef_ref[1:2, :], parts)
        match = slot == iota((ndev, terms), 0) * CAP + c
        message += product(jnp.where(match, 1.0, 0.0), parts, 1, 1, EXACT)
        number = jnp.max(jnp.where(match, block, -1.0), axis=1, keepdims=True)
        message = jnp.where(lane == base + 9, number, message)
    msg_send[...] = message.reshape(ndev, 1, 128)

    each(ncol, lambda t: orb_copy(t).start())
    each(ndev, lambda t: msg_copy(t).start())

    for c in range(1, len(chunks)):
        add_slots(c)
        each(ndev, lambda t: exch_copy(c, t).start())
        own_copy(c).start()

    each(ncol, lambda t: orb_copy(t).wait())
    all_orb[q] = orb_send[...]
    each(ndev, lambda t: msg_copy(t).wait())
    msg_recv[me] = msg_send[me]

    wide = all_orb[...].astype(f32)
    orbs = jnp.concatenate(
        [
            wide[:, :orb_rows, :].reshape(ncol * orb_rows, points // 2),
            wide[:, orb_rows:, :].reshape(ncol * orb_rows, points // 2),
        ],
        axis=1,
    ).astype(bf16)
    chan_row = chan_ref[...]
    chan_place = chan_row // orb_per * orb_rows + chan_row % orb_per
    owns = jnp.where(iota((ncol * orb_rows, chans), 0) == chan_place, 1.0, 0.0).astype(bf16)
    number = iota((128, chans), 0)
    first_chan = number // BAND * nrow + p
    second_chan = (first_chan // ncol + number % BAND) % groups * ncol + q

    def orbital_of(chan):
        hot = jnp.where(iota((128, chans), 1) == chan, 1.0, 0.0).astype(bf16)
        return product(product(hot, owns, 1, 1).astype(bf16), orbs, 1, 0)

    received = msg_recv[...].reshape(ndev, 128)
    numbers = []
    sums = jnp.zeros((128, 128), f32)
    for c in range(CAP):
        base = SPAN * c
        ids = jnp.sum(jnp.where(lane == base + 9, received, 0.0), axis=1, keepdims=True)
        numbers.append(ids)
        hot = jnp.where(lane.astype(f32) == ids, 1.0, 0.0)
        inside = (lane >= base) & (lane < base + 9)
        sums += product(hot, jnp.where(inside, received, 0.0), 0, 0, EXACT)
    pot_pad[...] = jnp.zeros_like(pot_pad)
    for c in range(CAP):
        pot_pad[SPAN * c : SPAN * c + 8, :] = pot_ref[...]
    lanes = iota((128, 128), 1)
    factor = jnp.sum(jnp.where(lanes % SPAN == 8, sums, 0.0), axis=1, keepdims=True)
    weights[...] = product(sums, pot_pad[...], 1, 0, EXACT) + factor * (
        orbital_of(first_chan) * orbital_of(second_chan)
    )

    size = lists.shape[1]
    source = iota((ndev, size), 0)
    spot = iota((ndev, size), 1)
    row = jnp.full((1, size), -1.0, f32)
    for c in range(CAP):
        row += jnp.sum(
            jnp.where(spot == source * CAP + c, numbers[c] + 1.0, 0.0), axis=0, keepdims=True
        )
    col = turned(row)
    under = iota((size, size), 0).astype(f32)
    over = iota((size, size), 1).astype(f32)
    heads = jnp.min(jnp.where(col == over, under, FAR), axis=0, keepdims=True)
    nexts = jnp.min(jnp.where((col == row) & (under > over), under, FAR), axis=0, keepdims=True)
    lists[...] = jnp.zeros_like(lists)
    lists[0:1, :] = jnp.where(heads < FAR, heads, -1.0).astype(jnp.int32)
    lists[1:2, :] = jnp.where(nexts < FAR, nexts, -1.0).astype(jnp.int32)

    lists_copy = pltpu.make_async_copy(lists, lists_ref, own_sem.at[7])
    lists_copy.start()
    basis_t[...] = basis_ref[...].astype(f32).T

    def form(t, carried):
        scaled = (basis_t[...] * weights[pl.ds(t, 1), :]).astype(bf16)
        local_ref[t] = jnp.dot(
            scaled, basis_ref[...], preferred_element_type=f32
        ).astype(bf16)
        return carried

    lax.fori_loop(0, blocks, form, 0)
    for c in range(len(chunks)):
        each(ndev, lambda t: exch_copy(c, t).wait())
        own_copy(c).wait()
    lists_copy.wait()


def exchange(nrow, ncol, exchange_ops, orbitals, potentials, chan, slot, pairs, coefs, basis):
    ndev = nrow * ncol
    terms, inner, width = exchange_ops.shape
    points = basis.shape[0]
    blocks = RBLK * BAND
    orb_rows = -(-orbitals.shape[0] // 8) * 8
    size = -(-max(ndev * CAP, 128) // 128) * 128
    span = -(-max(ndev * CAP, terms) // 128) * 128
    heights = BANDS + (inner - sum(BANDS),)
    near = ndev * CAP * inner * width * 2 <= NEAR_BYTES
    place = pltpu.VMEM if near else jax.ShapeDtypeStruct
    any_spec = pl.BlockSpec(memory_space=pl.ANY)
    smem = pl.BlockSpec(memory_space=pltpu.SMEM)
    vmem = pl.BlockSpec(memory_space=pltpu.VMEM)
    dma = pltpu.SemaphoreType.DMA
    f32, bf16 = jnp.float32, jnp.bfloat16
    return pl.pallas_call(
        functools.partial(exchange_kernel, nrow, ncol),
        out_shape=(
            place((ndev, CAP, inner, width), bf16),
            pltpu.VMEM((blocks, width, width), bf16),
            pltpu.SMEM((8, size), jnp.int32),
        ),
        in_specs=[any_spec] + [vmem] * 7,
        out_specs=(vmem if near else any_spec, vmem, smem),
        scratch_shapes=[
            *[pltpu.VMEM((terms, rows, width), bf16) for rows in heights],
            pltpu.VMEM((terms, max(heights), width), bf16),
            *[pltpu.VMEM((ndev, CAP, rows, width), bf16) for rows in heights],
            pltpu.VMEM((8, size), jnp.int32),
            pltpu.VMEM((orb_rows, points), f32),
            pltpu.VMEM((2 * orb_rows, points // 2), bf16),
            pltpu.VMEM((ncol, 2 * orb_rows, points // 2), bf16),
            pltpu.VMEM((ndev, 1, 128), f32),
            pltpu.VMEM((ndev, 1, 128), f32),
            pltpu.VMEM((128, points), f32),
            pltpu.VMEM((width, points), f32),
            pltpu.VMEM((128, points), f32),
            pltpu.VMEM((8, span), jnp.int32),
            pltpu.SMEM((8, span), jnp.int32),
            dma((ncol,)),
            dma((ncol,)),
            dma((ndev,)),
            dma((ndev,)),
            dma((3, ndev)),
            dma((3, ndev)),
            dma((8,)),
        ],
        compiler_params=pltpu.CompilerParams(
            collective_id=0, has_side_effects=True, vmem_limit_bytes=EXCHANGE_BYTES
        ),
        name="exchange",
    )(exchange_ops, orbitals, potentials, chan, slot, pairs, coefs, basis)


def blocks_kernel(
    lists_smem,
    recv_ref,
    basis_ref,
    local_ref,
    out_ref,
    inner_t,
    sums,
    joined_a,
    joined_b,
    formed,
    sems,
):
    f32 = jnp.float32
    steps = local_ref.shape[0] // BLOCKS_STEP
    inner_t[...] = basis_ref[: recv_ref.shape[1], :].astype(f32).T.astype(jnp.bfloat16)

    def leave(step):
        span = pl.ds(step * BLOCKS_STEP, BLOCKS_STEP)
        return pltpu.make_async_copy(formed.at[span], out_ref.at[span], sems.at[step])

    def slots_of(step, i):
        head = lists_smem[0, step * BLOCKS_STEP + i]
        follower = jnp.where(head < 0, -1, lists_smem[1, jnp.maximum(head, 0)])
        third = jnp.where(follower < 0, -1, lists_smem[1, jnp.maximum(follower, 0)])
        return head, follower, third

    def join(step, joined, i):
        head, follower, third = slots_of(step, i)
        one = recv_ref[jnp.maximum(head, 0)]
        two = recv_ref[jnp.maximum(follower, 0)]
        nothing = jnp.zeros_like(one)
        joined[i] = jnp.where(head < 0, nothing, one) + jnp.where(follower < 0, nothing, two)
        return third

    def multiply(step, joined, i):
        t = step * BLOCKS_STEP + i
        swapped = jnp.dot(inner_t[...], joined[i], preferred_element_type=f32)
        formed[t] = (swapped + local_ref[t].astype(f32)).astype(formed.dtype)

    def join_long(step, joined, longest):
        @pl.when(longest >= 0)
        def _():
            def rejoin(i, c):
                head, follower, third = slots_of(step, i)

                @pl.when(third >= 0)
                def _():
                    sums[...] = recv_ref[head].astype(f32) + recv_ref[follower].astype(f32)

                    def more(s):
                        sums[...] += recv_ref[s].astype(f32)
                        after = lists_smem[1, s]
                        return jnp.where(after > s, after, -1)

                    lax.while_loop(lambda s: s >= 0, more, third)
                    joined[i] = sums[...].astype(joined.dtype)

                return c

            lax.fori_loop(0, BLOCKS_STEP, rejoin, 0)

    def work(step, now, later):
        following = jnp.minimum(step + 1, steps - 1)
        longest = jnp.int32(-1)
        for i in range(BLOCKS_STEP):
            multiply(step, now, i)
            longest = jnp.maximum(longest, join(following, later, i))
        leave(step).start()
        join_long(following, later, longest)

    def work_pair(pair, carried):
        work(2 * pair, joined_a, joined_b)
        work(2 * pair + 1, joined_b, joined_a)
        return carried

    longest = jnp.int32(-1)
    for i in range(BLOCKS_STEP):
        longest = jnp.maximum(longest, join(0, joined_a, i))
    join_long(0, joined_a, longest)
    lax.fori_loop(0, steps // 2, work_pair, 0)

    def finish(step, carried):
        leave(step).wait()
        return carried

    lax.fori_loop(0, steps, finish, 0)


def make_blocks(lists, received, local, basis):
    slots, inner, width = received.shape
    blocks = local.shape[0]
    vmem = pl.BlockSpec(memory_space=pltpu.VMEM)
    return pl.pallas_call(
        blocks_kernel,
        in_specs=[
            pl.BlockSpec(memory_space=pltpu.SMEM),
            vmem,
            vmem,
            vmem,
        ],
        out_specs=pl.BlockSpec(memory_space=pl.ANY),
        scratch_shapes=[
            pltpu.VMEM((width, inner), jnp.bfloat16),
            pltpu.VMEM((inner, width), jnp.float32),
            pltpu.VMEM((BLOCKS_STEP, inner, width), jnp.bfloat16),
            pltpu.VMEM((BLOCKS_STEP, inner, width), jnp.bfloat16),
            pltpu.VMEM((blocks, width, width), jnp.bfloat16),
            pltpu.SemaphoreType.DMA((blocks // BLOCKS_STEP,)),
        ],
        out_shape=jax.ShapeDtypeStruct((blocks, width, width), jnp.bfloat16),
        compiler_params=pltpu.CompilerParams(vmem_limit_bytes=BLOCKS_BYTES),
        name="make_blocks",
    )(lists, received, basis, local)


def on_device(basis, potentials, orbitals, chan_orbital, pair_list, slot_list, coefs, exchange_ops):
    nrow = lax.axis_size("prow")
    ncol = lax.axis_size("pcol")
    inner, width = exchange_ops.shape[1:]
    received, local, lists = exchange(
        nrow,
        ncol,
        exchange_ops,
        orbitals,
        potentials,
        chan_orbital[None, :],
        slot_list[None, :],
        pair_list.T,
        coefs.T,
        basis,
    )
    blocks = make_blocks(lists, received.reshape(-1, inner, width), local, basis)
    return blocks.reshape(RBLK, 1, BAND, 1, width, width)


def solution(mesh):
    placed = (
        P(),
        P(),
        P("pcol", None),
        P(),
        P(("prow", "pcol"), None),
        P(("prow", "pcol")),
        P(("prow", "pcol"), None),
        P(("prow", "pcol"), None, None),
    )
    return jax.shard_map(
        on_device,
        mesh=mesh,
        in_specs=placed,
        out_specs=P(None, "prow", None, "pcol", None, None),
        check_vma=False,
    )
```
